256 devices in a mesh: prompt: 8 (over z_hi, x), seq: 32 (over y, z_lo, core).
Axes of the slice: x: 4, y: 4, z: 8 (z_hi: 2, z_lo: 4; z = z_hi * 4 + z_lo), core: 2. Of those that a mesh axis runs over, the one named last changes fastest.
Arguments:
- queries: bfloat16 [8, 2, 1536, 8192], P('prompt', None, 'seq'), as said below
- resp_kv: bfloat16 [8, 2, 1536, 2048], P('prompt', None, 'seq'), as said below
- prompt_kv: bfloat16 [8, 1024, 2048], P(None, 'seq', 'prompt'), may hold values from -6 to 6
- block_order: int32 [8, 32], P('prompt'), may hold values from 0 to 31, each once within a row
- prompt_len: int32 [8], P('prompt'), may hold values from 256 to 1024, as said below
- resp_len: int32 [8, 2], P('prompt'), may hold values from 384 to 1536, as said below
Outputs:
- attended: bfloat16 [8, 2, 1536, 8192], P('prompt', None, 'seq')
The draws below stay inside these ranges and needn't reach their ends.
Inputs may be any that keep to these rules, and one draw needn't show every extreme that they name: `prompt_len`: at least 256; one prompt has exactly 1024. `resp_len`: at least 384; one response has exactly 1536. `block_order`: each row names every storage block's prompt block once. `queries`: real values. `resp_kv`: real values.
All inputs are finite; a program needn't handle non-finite values.
Results may differ from the reference program's by a relative error of at most 0.008.
Values may be sent and summed in bfloat16 or wider, within the bound.
A program may use at most 128 MiB of HBM per device.

```python
import math
import jax
import jax.numpy as jnp
from jax import lax

H = 64
KVH = 8
HD = 128
CP = 32
PROMPTS = 8
LR = 1536
LP = 1024
N_SEQ = 32


def shared_keys(key):
    return jax.random.normal(key, (PROMPTS, 2, LR, KVH * 2 * HD), jnp.float32)


def draw_resp_kv(key, part):
    base = shared_keys(key)
    return jnp.clip(base, -6.0, 6.0).astype(jnp.bfloat16)


def draw_queries(key, part):
    key = jax.random.fold_in(key, 11)
    values = jax.random.normal(key, (PROMPTS, 2, LR, H * HD), jnp.float32)
    return values.astype(jnp.bfloat16)


def draw_prompt_len(key, part):
    key = jax.random.fold_in(key, 3)
    values = jax.random.randint(key, (PROMPTS,), LP // 4, LP + 1, jnp.int32)
    return values.at[0].set(LP)


def draw_resp_len(key, part):
    key = jax.random.fold_in(key, 5)
    values = jax.random.randint(key, (PROMPTS, 2), LR // 4, LR + 1, jnp.int32)
    return values.at[0, 1].set(LR)


def block_levels(key, dims, pieces, low, top_value):
    def one(axis_at, shards_of):
        heights = jax.random.uniform(jax.random.fold_in(jax.random.fold_in(key, 6), axis_at), (shards_of,), jnp.float32, low / len(pieces), top_value / len(pieces))
        return jnp.repeat(jnp.exp(heights), dims[axis_at] // shards_of).reshape((-1,) + (1,) * (len(dims) - axis_at - 1))

    level = one(*pieces[0])
    for cut in pieces[1:]:
        level = level * one(*cut)
    return level


def gaussian(rng, shape, deviation, most, cuts=(), kind=jnp.bfloat16):
    array = jax.random.normal(rng, shape, jnp.float32) * deviation
    if len(cuts) > 0:
        array = block_levels(rng, shape, cuts, -0.22, 0.18) * array
    return jnp.clip(array, min=-most, max=most).astype(kind)


def setup_inputs(seed: int = 0) -> dict:
    key_of = jax.random.split(jax.random.key(seed), 7)
    queries = draw_queries(jax.random.fold_in(key_of[6], 71), 0)
    resp_kv = draw_resp_kv(jax.random.fold_in(key_of[6], 71), 0)
    prompt_kv = gaussian(key_of[2], (PROMPTS, LP, KVH * 2 * HD), 1.0, 6.0, ((1, 32), (2, 8)))
    block_order = jax.vmap(lambda own: jax.random.permutation(own, N_SEQ))(jax.random.split(key_of[3], PROMPTS)).reshape((PROMPTS, N_SEQ)).astype(jnp.int32)
    prompt_len = draw_prompt_len(jax.random.fold_in(key_of[6], 71), 0)
    resp_len = draw_resp_len(jax.random.fold_in(key_of[6], 71), 0)
    return dict(queries=queries, resp_kv=resp_kv, prompt_kv=prompt_kv, block_order=block_order, prompt_len=prompt_len, resp_len=resp_len)


def one_prompt(inputs):
    query_all, resp_all, prompt_all, order_row, plen, rlen = inputs
    group = H // KVH
    rows = jnp.arange(LP, dtype=jnp.int32)
    position = order_row[rows // CP] * CP + rows % CP
    prompt_live = position < plen
    qpos = jnp.arange(LR, dtype=jnp.int32)
    resp_live = qpos[None, :] < rlen[:, None]
    causal = qpos[None, :] <= qpos[:, None]
    resp_mask = causal[None, :, :] & resp_live[:, None, :]
    scale = 1.0 / math.sqrt(HD)

    def one_head(head):
        kv_head = head // group
        query = lax.dynamic_slice_in_dim(query_all, head * HD, HD, 2).astype(jnp.float32)
        prompt_head = lax.dynamic_slice_in_dim(prompt_all, kv_head * 2 * HD, 2 * HD, 1).astype(jnp.float32)
        resp_head = lax.dynamic_slice_in_dim(resp_all, kv_head * 2 * HD, 2 * HD, 2).astype(jnp.float32)
        score_prompt = jnp.einsum('crd,kd->crk', query, prompt_head[:, :HD]) * scale
        score_resp = jnp.einsum('crd,ckd->crk', query, resp_head[:, :, :HD]) * scale
        pmask = prompt_live[None, None, :]
        score_prompt = jnp.where(pmask, score_prompt, -1e+30)
        score_resp = jnp.where(resp_mask, score_resp, -1e+30)
        best = jnp.maximum(lax.optimization_barrier(jnp.max(score_prompt, axis=-1)), lax.optimization_barrier(jnp.max(score_resp, axis=-1)))
        exp_prompt = jnp.where(pmask, jnp.exp(score_prompt - best[..., None]), 0.0)
        exp_resp = jnp.where(resp_mask, jnp.exp(score_resp - best[..., None]), 0.0)
        total = lax.optimization_barrier(jnp.sum(exp_prompt, axis=-1)) + lax.optimization_barrier(jnp.sum(exp_resp, axis=-1))
        weight_prompt = exp_prompt.astype(jnp.bfloat16).astype(jnp.float32)
        weight_resp = exp_resp.astype(jnp.bfloat16).astype(jnp.float32)
        summed = jnp.einsum('crk,kd->crd', weight_prompt, prompt_head[:, HD:])
        summed = summed + jnp.einsum('crk,ckd->crd', weight_resp, resp_head[:, :, HD:])
        result = summed / total[..., None] * resp_live[:, :, None].astype(jnp.float32)
        return result.astype(jnp.bfloat16)
    heads_out = lax.map(one_head, jnp.arange(H, dtype=jnp.int32))
    return jnp.transpose(heads_out, (1, 2, 0, 3)).reshape(2, LR, H * HD)

def reference(queries, resp_kv, prompt_kv, block_order, prompt_len, resp_len):
    return lax.map(one_prompt, (queries, resp_kv, prompt_kv, block_order, prompt_len, resp_len))
```

```python
import functools
import math

import jax
import jax.numpy as jnp
from jax import lax
from jax.experimental import pallas as pl
from jax.experimental.pallas import tpu as pltpu
from jax.sharding import PartitionSpec as P

H = 64
KVH = 8
HD = 128
CP = 32
NP = 8
NY, NZ, NC = 4, 4, 2
ROWS = 48
GROUP = H // KVH
QW = GROUP * HD
KVW = 2 * HD
SEG = NZ * NC * ROWS
RT = GROUP * NC * ROWS
PCH = 512
NPROMPT = NY * NZ * NC * CP
SCALE = math.log2(math.e) / math.sqrt(HD)
MESH = pl.DeviceIdType.MESH
NEG = -1e30


def kernel(
    q_in, r_in, p_in, order, plen, rlen, out,
    qbuf, rbuf, pbuf, obuf, kp, vp, sbuf, mbuf, accbuf, bias,
    q_s, q_r, r_s, r_r, p_s, p_r, zp_s, zp_r, zr_s, zr_r, o_s, o_r,
):
    p = lax.axis_index("prompt")
    s = lax.axis_index("seq")
    y = s // (NZ * NC)
    z = lax.rem(s, NZ * NC) // NC
    c = lax.rem(s, NC)
    mine = y * NC + c
    home = lax.div(p, NC) * (NZ * NC) + z * NC + lax.rem(p, NC)

    def seq_of(index, zz):
        return lax.div(index, NC) * (NZ * NC) + zz * NC + lax.rem(index, NC)

    def at_rel(k):
        return lax.rem(mine + k, NY * NC)

    def remote(src, dst, ss, rs, dev):
        return pltpu.make_async_remote_copy(
            src_ref=src, dst_ref=dst, send_sem=ss, recv_sem=rs, device_id=dev, device_id_type=MESH
        )

    def landed(ref, sem):
        pltpu.make_async_copy(ref, ref, sem).wait()

    barrier = pltpu.get_barrier_semaphore()

    def greet(dev):
        pl.semaphore_signal(barrier, inc=1, device_id=dev, device_id_type=MESH)

    for k in range(1, NY * NC):
        greet((p, seq_of(at_rel(k), z)))
    for k in range(1, NZ):
        greet((p, y * (NZ * NC) + lax.rem(z + k, NZ) * NC + c))
    for k in range(1, NP):
        greet((lax.rem(p + k, NP), home))
    for k in range(1, NY * NC):
        greet((mine, seq_of(at_rel(k), z)))

    @pl.when(p != mine)
    def _():
        greet((p, home))
        greet((mine, s))

    extra = jnp.where(p != mine, 2, 0)
    pl.semaphore_wait(barrier, (NY * NC - 1) * 2 + (NZ - 1) + (NP - 1) + extra)

    def r_copy(k):
        t = at_rel(k)
        src = r_in.at[0, :, :, pl.ds(pl.multiple_of(t * KVW, KVW), KVW)]
        dst = rbuf.at[:, y, z, c]
        if k == 0:
            return pltpu.make_async_copy(src, dst, r_r.at[mine])
        return remote(src, dst, r_s.at[k], r_r.at[mine], (p, seq_of(t, z)))

    def q_copy(k):
        t = at_rel(k)
        src = q_in.at[0, :, :, pl.ds(pl.multiple_of(t * QW, QW), QW)]
        dst = qbuf.at[y, c]
        if k == 0:
            return pltpu.make_async_copy(src, dst, q_r.at[mine])
        return remote(src, dst, q_s.at[k], q_r.at[mine], (p, seq_of(t, z)))

    def p_copy(k):
        t = lax.rem(p + k, NP)
        return remote(p_in.at[t], pbuf.at[y, z, c], p_s.at[k], p_r.at[mine], (t, home))

    def p_local():
        return pltpu.make_async_copy(p_in.at[p], pbuf.at[y, z, c], p_r.at[mine])

    for k in range(1, NP):
        p_copy(k).start()

    @pl.when(p != mine)
    def _():
        p_copy(0).start()

    @pl.when(p == mine)
    def _():
        p_local().start()

    for k in range(NY * NC):
        r_copy(k).start()
    for k in range(NY * NC):
        q_copy(k).start()

    def z_dev(zz):
        return (p, y * (NZ * NC) + zz * NC + c)

    def zp_copy(src_z, dst_z, slot):
        ref = pbuf.at[:, src_z]
        return remote(ref, ref, zp_s.at[slot], zp_r.at[src_z], z_dev(dst_z))

    def zr_copy(g, src_z, dst_z, slot):
        ref = rbuf.at[:, g, src_z]
        return remote(ref, ref, zr_s.at[g, slot], zr_r.at[g, src_z], z_dev(dst_z))

    def each_near(act):
        for slot, dz in enumerate((1, -1, 2, -2)):
            @pl.when(jnp.logical_and(z + dz >= 0, z + dz < NZ))
            def _(slot=slot, dz=dz):
                act(slot, z + dz)

    middle = jnp.logical_and(z > 0, z < NZ - 1)
    far_dst = (z - 1) * (NZ - 1)
    far_src = (NZ - 1) - far_dst

    for i in range(NY):
        for j in range(NC):
            landed(pbuf.at[i, z, j], p_r.at[i * NC + j])
    each_near(lambda slot, dz: zp_copy(z, dz, slot).start())
    for i in range(NY):
        for j in range(NC):
            landed(rbuf.at[:, i, z, j], r_r.at[i * NC + j])
        each_near(lambda slot, dz, i=i: zr_copy(i, z, dz, slot).start())

    @pl.when(middle)
    def _():
        landed(pbuf.at[:, far_src], zp_r.at[far_src])
        zp_copy(far_src, far_dst, 4).start()

    def relay_resp(i):
        @pl.when(middle)
        def _():
            landed(rbuf.at[:, i, far_src], zr_r.at[i, far_src])
            zr_copy(i, far_src, far_dst, 4).start()

    relay_resp(0)

    row_at = lax.broadcasted_iota(jnp.int32, (NC * ROWS, SEG), 0) + z * (NC * ROWS)
    col_at = lax.broadcasted_iota(jnp.int32, (NC * ROWS, SEG), 1)
    bias[...] = jnp.where(col_at <= row_at, 0.0, NEG)

    def wait_z(ref_of, sem_of):
        for k in range(1, NZ):
            src = lax.rem(z + k, NZ)
            relayed = jnp.logical_and(middle, src == far_src)

            @pl.when(jnp.logical_not(relayed))
            def _():
                landed(ref_of(src), sem_of(src))

    wait_z(lambda zz: pbuf.at[:, zz], lambda zz: zp_r.at[zz])

    positions = []
    for i in range(NY * NZ * NC):
        positions.append(order[0, i] * CP + lax.broadcasted_iota(jnp.int32, (CP, HD), 0))
    position = jnp.concatenate(positions, axis=0)
    live = position < plen[0]
    whole = pbuf[...].reshape(NPROMPT, KVW)
    keys = whole[:, :HD].astype(jnp.float32)
    vals = whole[:, HD:].astype(jnp.float32)
    first = jnp.sum(jnp.where(position == 0, keys, 0.0), axis=0, keepdims=True)
    kp[...] = jnp.where(live, keys, first).astype(jnp.bfloat16)
    vp[:, :HD] = jnp.where(live, vals, 0.0).astype(jnp.bfloat16)
    vp[:, HD:] = jnp.where(live, 1.0, 0.0).astype(jnp.bfloat16)

    dims = (((1,), (1,)), ((), ()))

    def lane_max(x):
        best = x[:, :HD]
        for t in range(1, x.shape[1] // HD):
            best = jnp.maximum(best, x[:, t * HD : (t + 1) * HD])
        return best

    def attend(g, cand):
        def q_rows():
            block = qbuf[g, :, cand]
            return jnp.concatenate(
                [block[:, :, h * HD : (h + 1) * HD].reshape(NC * ROWS, HD) for h in range(GROUP)], axis=0
            )

        mbuf[...] = jnp.full((RT, HD), NEG, jnp.float32)

        def score_prompt(t, _):
            at = pl.multiple_of(t * PCH, PCH)
            sc = lax.dot_general(q_rows(), kp[pl.ds(at, PCH), :], dims, preferred_element_type=jnp.float32)
            sbuf[:, pl.ds(at, PCH)] = sc
            mbuf[...] = jnp.maximum(mbuf[...], lane_max(sc))
            return 0

        lax.fori_loop(0, NPROMPT // PCH, score_prompt, 0)

        def resp_keys(t):
            return rbuf[cand, t].reshape(SEG, KVW)

        def score_resp(t, _):
            at = pl.multiple_of(NPROMPT + t * SEG, HD)
            sc = lax.dot_general(q_rows(), resp_keys(t)[:, :HD], dims, preferred_element_type=jnp.float32)
            sbuf[:, pl.ds(at, SEG)] = sc
            mbuf[...] = jnp.maximum(mbuf[...], lane_max(sc))
            return 0

        lax.fori_loop(0, g, score_resp, 0)
        at = pl.multiple_of(NPROMPT + g * SEG, HD)
        sc = lax.dot_general(q_rows(), resp_keys(g)[:, :HD], dims, preferred_element_type=jnp.float32)
        sc = (sc.reshape(GROUP, NC * ROWS, SEG) + bias[...][None]).reshape(RT, SEG)
        sbuf[:, pl.ds(at, SEG)] = sc
        best = jnp.max(jnp.maximum(mbuf[...], lane_max(sc)), axis=1, keepdims=True) * SCALE
        mbuf[...] = jnp.broadcast_to(best, (RT, HD))
        accbuf[...] = jnp.zeros((RT, KVW), jnp.float32)

        def weights(at, size):
            m = mbuf[...]
            m = jnp.concatenate([m] * (size // HD), axis=1)
            return jnp.exp2(sbuf[:, pl.ds(at, size)] * SCALE - m).astype(jnp.bfloat16)

        def add_prompt(t, _):
            at = pl.multiple_of(t * PCH, PCH)
            accbuf[...] += jnp.dot(weights(at, PCH), vp[pl.ds(at, PCH), :], preferred_element_type=jnp.float32)
            return 0

        lax.fori_loop(0, NPROMPT // PCH, add_prompt, 0)

        def add_resp(t, _):
            at = pl.multiple_of(NPROMPT + t * SEG, HD)
            vx = jnp.concatenate([resp_keys(t)[:, HD:], jnp.ones((SEG, HD), jnp.bfloat16)], axis=1)
            accbuf[...] += jnp.dot(weights(at, SEG), vx, preferred_element_type=jnp.float32)
            return 0

        lax.fori_loop(0, g + 1, add_resp, 0)
        acc = accbuf[...]
        res = (acc[:, :HD] / acc[:, HD:]).reshape(GROUP, NC * ROWS, HD)
        pos = lax.broadcasted_iota(jnp.int32, (NC * ROWS, HD), 0) + (g * SEG + z * (NC * ROWS))
        alive = pos < rlen[0, cand]
        for h in range(GROUP):
            piece = jnp.where(alive, res[h], 0.0).astype(jnp.bfloat16)
            obuf[g, :, cand, :, h * HD : (h + 1) * HD] = piece.reshape(NC, ROWS, HD)

    out_ref = out.at[0, :, :, pl.ds(pl.multiple_of(mine * QW, QW), QW)]

    def o_remote(g, j):
        return remote(obuf.at[g, j], out_ref, o_s.at[g, j], o_r.at[mine], (p, seq_of(g * NC + j, z)))

    def o_local(g, j):
        return pltpu.make_async_copy(obuf.at[g, j], out_ref, o_r.at[mine])

    def group_step(g, _):
        for j in range(NC):
            landed(qbuf.at[g, j], q_r.at[g * NC + j])
        wait_z(lambda zz: rbuf.at[:, g, zz], lambda zz: zr_r.at[g, zz])

        attend(g, 0)

        @pl.when(g < NY - 1)
        def _():
            relay_resp(g + 1)

        attend(g, 1)

        for j in range(NC):
            @pl.when(g * NC + j == mine)
            def _():
                o_local(g, j).start()

            @pl.when(g * NC + j != mine)
            def _():
                o_remote(g, j).start()
        return 0

    lax.fori_loop(0, NY, group_step, 0)

    for k in range(1, NY * NC):
        q_copy(k).wait_send()
        r_copy(k).wait_send()
        p_copy(k).wait_send()

    @pl.when(p != mine)
    def _():
        p_copy(0).wait_send()

    each_near(lambda slot, dz: zp_copy(z, dz, slot).wait_send())
    for i in range(NY):
        each_near(lambda slot, dz, i=i: zr_copy(i, z, dz, slot).wait_send())

    @pl.when(middle)
    def _():
        zp_copy(far_src, far_dst, 4).wait_send()
        for i in range(NY):
            zr_copy(i, far_src, far_dst, 4).wait_send()

    for i in range(NY):
        for j in range(NC):
            @pl.when(i * NC + j != mine)
            def _(i=i, j=j):
                o_remote(i, j).wait_send()

    for k in range(NY * NC):
        landed(out.at[0, :, :, pl.ds(k * QW, QW)], o_r.at[k])


def shards(queries, resp_kv, prompt_kv, block_order, prompt_len, resp_len):
    bf16, f32 = jnp.bfloat16, jnp.float32
    dma = pltpu.SemaphoreType.DMA
    any_spec = pl.BlockSpec(memory_space=pl.ANY)
    smem = pl.BlockSpec(memory_space=pltpu.SMEM)
    return pl.pallas_call(
        kernel,
        out_shape=jax.ShapeDtypeStruct(queries.shape, bf16),
        in_specs=[any_spec] * 3 + [smem] * 3,
        out_specs=any_spec,
        scratch_shapes=[
            pltpu.VMEM((NY, NC, 2, ROWS, QW), bf16),
            pltpu.VMEM((2, NY, NZ, NC, ROWS, KVW), bf16),
            pltpu.VMEM((NY, NZ, NC, CP, KVW), bf16),
            pltpu.VMEM((NY, NC, 2, ROWS, QW), bf16),
            pltpu.VMEM((NPROMPT, HD), bf16),
            pltpu.VMEM((NPROMPT, KVW), bf16),
            pltpu.VMEM((RT, NPROMPT + NY * SEG), f32),
            pltpu.VMEM((RT, HD), f32),
            pltpu.VMEM((RT, KVW), f32),
            pltpu.VMEM((NC * ROWS, SEG), f32),
            dma((NY * NC,)), dma((NY * NC,)),
            dma((NY * NC,)), dma((NY * NC,)),
            dma((NP,)), dma((NY * NC,)),
            dma((5,)), dma((NZ,)),
            dma((NY, 5)), dma((NY, NZ)),
            dma((NY, NC)), dma((NY * NC,)),
        ],
        compiler_params=pltpu.CompilerParams(
            collective_id=0, has_side_effects=True, vmem_limit_bytes=48 * 1024 * 1024
        ),
        name="attend",
    )(queries, resp_kv, prompt_kv, block_order, prompt_len, resp_len)


def solution(mesh):
    in_specs = (
        P("prompt", None, "seq", None),
        P("prompt", None, "seq", None),
        P(None, "seq", "prompt"),
        P("prompt", None),
        P("prompt"),
        P("prompt", None),
    )
    out_specs = P("prompt", None, "seq", None)
    return jax.shard_map(shards, mesh=mesh, in_specs=in_specs, out_specs=out_specs, check_vma=False)
```

```python
import functools
import math

import jax
import jax.numpy as jnp
from jax import lax
from jax.experimental import pallas as pl
from jax.experimental.pallas import tpu as pltpu
from jax.sharding import PartitionSpec as P

H = 64
KVH = 8
HD = 128
CP = 32
NP = 8
NY, NZ, NC = 4, 4, 2
ROWS = 48
GROUP = H // KVH
QW = GROUP * HD
KVW = 2 * HD
SEG = NZ * NC * ROWS
RT = GROUP * NC * ROWS
PCH = 512
NPROMPT = NY * NZ * NC * CP
SCALE = math.log2(math.e) / math.sqrt(HD)
MESH = pl.DeviceIdType.MESH
NEG = -1e30
UNITS = 2 * NY
AHEAD = 2


def kernel(
    q_in, r_in, p_in, order, plen, rlen, out,
    qbuf, rbuf, pbuf, obuf, kp, vp, sbuf, mbuf, accbuf, bias,
    q_s, q_r, r_s, r_r, p_s, p_r, zp_s, zp_r, zr_s, zr_r, o_s, o_r,
):
    p = lax.axis_index("prompt")
    s = lax.axis_index("seq")
    y = s // (NZ * NC)
    z = lax.rem(s, NZ * NC) // NC
    c = lax.rem(s, NC)
    mine = y * NC + c
    home = lax.div(p, NC) * (NZ * NC) + z * NC + lax.rem(p, NC)

    def seq_of(index, zz):
        return lax.div(index, NC) * (NZ * NC) + zz * NC + lax.rem(index, NC)

    def at_rel(k):
        return lax.rem(mine + k, NY * NC)

    def remote(src, dst, ss, rs, dev):
        return pltpu.make_async_remote_copy(
            src_ref=src, dst_ref=dst, send_sem=ss, recv_sem=rs, device_id=dev, device_id_type=MESH
        )

    def landed(ref, sem):
        pltpu.make_async_copy(ref, ref, sem).wait()

    barrier = pltpu.get_barrier_semaphore()

    def greet(dev):
        pl.semaphore_signal(barrier, inc=1, device_id=dev, device_id_type=MESH)

    for k in range(1, NY * NC):
        greet((p, seq_of(at_rel(k), z)))
    for k in range(1, NZ):
        greet((p, y * (NZ * NC) + lax.rem(z + k, NZ) * NC + c))
    for k in range(1, NP):
        greet((lax.rem(p + k, NP), home))
    for k in range(1, NY * NC):
        greet((mine, seq_of(at_rel(k), z)))

    @pl.when(p != mine)
    def _():
        greet((p, home))
        greet((mine, s))

    extra = jnp.where(p != mine, 2, 0)
    pl.semaphore_wait(barrier, (NY * NC - 1) * 2 + (NZ - 1) + (NP - 1) + extra)

    def r_copy(k):
        t = at_rel(k)
        src = r_in.at[0, :, :, pl.ds(pl.multiple_of(t * KVW, KVW), KVW)]
        dst = rbuf.at[:, y, z, c]
        if k == 0:
            return pltpu.make_async_copy(src, dst, r_r.at[mine])
        return remote(src, dst, r_s.at[k], r_r.at[mine], (p, seq_of(t, z)))

    def q_copy(k, cand):
        t = at_rel(k)
        src = q_in.at[0, cand, :, pl.ds(pl.multiple_of(t * QW, QW), QW)]
        dst = qbuf.at[cand, y, c]
        if k == 0:
            return pltpu.make_async_copy(src, dst, q_r.at[cand, mine])
        return remote(src, dst, q_s.at[cand, k], q_r.at[cand, mine], (p, seq_of(t, z)))

    def p_copy(k):
        t = lax.rem(p + k, NP)
        return remote(p_in.at[t], pbuf.at[y, z, c], p_s.at[k], p_r.at[mine], (t, home))

    def p_local():
        return pltpu.make_async_copy(p_in.at[p], pbuf.at[y, z, c], p_r.at[mine])

    for k in range(1, NP):
        p_copy(k).start()

    @pl.when(p != mine)
    def _():
        p_copy(0).start()

    @pl.when(p == mine)
    def _():
        p_local().start()

    for k in range(NY * NC):
        r_copy(k).start()
    for cand in range(2):
        for k in range(NY * NC):
            q_copy(k, cand).start()

    def z_dev(zz):
        return (p, y * (NZ * NC) + zz * NC + c)

    def zp_copy(src_z, dst_z, slot):
        ref = pbuf.at[:, src_z]
        return remote(ref, ref, zp_s.at[slot], zp_r.at[src_z], z_dev(dst_z))

    def zr_copy(u, src_z, dst_z, slot):
        ref = rbuf.at[u // NY, u % NY, src_z]
        return remote(ref, ref, zr_s.at[u, slot], zr_r.at[u, src_z], z_dev(dst_z))

    middle = jnp.logical_and(z > 0, z < NZ - 1)
    far_dst = (z - 1) * (NZ - 1)
    far_src = (NZ - 1) - far_dst

    def each_near(act, early, late):
        for slot, dz in enumerate((1, -1, 2, -2)):
            there = jnp.logical_and(z + dz >= 0, z + dz < NZ)
            held = jnp.logical_and(middle, z + dz == far_dst)
            want = there
            if not early:
                want = jnp.logical_and(there, held)
            if not late:
                want = jnp.logical_and(there, jnp.logical_not(held))

            @pl.when(want)
            def _(slot=slot, dz=dz):
                act(slot, z + dz)

    def send_unit(u, early, late):
        each_near(lambda slot, dz: zr_copy(u, z, dz, slot).start(), early, late)

    for i in range(NY):
        for j in range(NC):
            landed(pbuf.at[i, z, j], p_r.at[i * NC + j])
    each_near(lambda slot, dz: zp_copy(z, dz, slot).start(), True, True)
    for i in range(NY):
        for j in range(NC):
            landed(rbuf.at[:, i, z, j], r_r.at[i * NC + j])
    for u in range(UNITS):
        send_unit(u, True, u < AHEAD)

    def relay_resp(u):
        @pl.when(middle)
        def _():
            landed(rbuf.at[u // NY, u % NY, far_src], zr_r.at[u, far_src])
            zr_copy(u, far_src, far_dst, 4).start()

        @pl.when(u + AHEAD < UNITS)
        def _():
            send_unit(u + AHEAD, False, True)

    @pl.when(middle)
    def _():
        landed(pbuf.at[:, far_src], zp_r.at[far_src])
        zp_copy(far_src, far_dst, 4).start()

    relay_resp(0)

    row_at = lax.broadcasted_iota(jnp.int32, (NC * ROWS, SEG), 0) + z * (NC * ROWS)
    col_at = lax.broadcasted_iota(jnp.int32, (NC * ROWS, SEG), 1)
    bias[...] = jnp.where(col_at <= row_at, 0.0, NEG)

    def wait_z(ref_of, sem_of):
        for k in range(1, NZ):
            src = lax.rem(z + k, NZ)
            relayed = jnp.logical_and(middle, src == far_src)

            @pl.when(jnp.logical_not(relayed))
            def _():
                landed(ref_of(src), sem_of(src))

    wait_z(lambda zz: pbuf.at[:, zz], lambda zz: zp_r.at[zz])

    positions = []
    for i in range(NY * NZ * NC):
        positions.append(order[0, i] * CP + lax.broadcasted_iota(jnp.int32, (CP, HD), 0))
    position = jnp.concatenate(positions, axis=0)
    live = position < plen[0]
    whole = pbuf[...].reshape(NPROMPT, KVW)
    keys = whole[:, :HD].astype(jnp.float32)
    vals = whole[:, HD:].astype(jnp.float32)
    first = jnp.sum(jnp.where(position == 0, keys, 0.0), axis=0, keepdims=True)
    kp[...] = jnp.where(live, keys, first).astype(jnp.bfloat16)
    vp[:, :HD] = jnp.where(live, vals, 0.0).astype(jnp.bfloat16)
    vp[:, HD:] = jnp.where(live, 1.0, 0.0).astype(jnp.bfloat16)

    dims = (((1,), (1,)), ((), ()))

    def lane_max(x):
        best = x[:, :HD]
        for t in range(1, x.shape[1] // HD):
            best = jnp.maximum(best, x[:, t * HD : (t + 1) * HD])
        return best

    def attend(u):
        cand, g = u // NY, lax.rem(u, NY)

        def q_rows():
            block = qbuf[cand, g]
            return jnp.concatenate(
                [block[:, :, h * HD : (h + 1) * HD].reshape(NC * ROWS, HD) for h in range(GROUP)], axis=0
            )

        mbuf[...] = jnp.full((RT, HD), NEG, jnp.float32)

        def score_prompt(t, _):
            at = pl.multiple_of(t * PCH, PCH)
            sc = lax.dot_general(q_rows(), kp[pl.ds(at, PCH), :], dims, preferred_element_type=jnp.float32)
            sbuf[:, pl.ds(at, PCH)] = sc
            mbuf[...] = jnp.maximum(mbuf[...], lane_max(sc))
            return 0

        lax.fori_loop(0, NPROMPT // PCH, score_prompt, 0)

        def resp_keys(t):
            return rbuf[cand, t].reshape(SEG, KVW)

        def score_resp(t, _):
            at = pl.multiple_of(NPROMPT + t * SEG, HD)
            sc = lax.dot_general(q_rows(), resp_keys(t)[:, :HD], dims, preferred_element_type=jnp.float32)
            sbuf[:, pl.ds(at, SEG)] = sc
            mbuf[...] = jnp.maximum(mbuf[...], lane_max(sc))
            return 0

        lax.fori_loop(0, g, score_resp, 0)
        at = pl.multiple_of(NPROMPT + g * SEG, HD)
        sc = lax.dot_general(q_rows(), resp_keys(g)[:, :HD], dims, preferred_element_type=jnp.float32)
        sc = (sc.reshape(GROUP, NC * ROWS, SEG) + bias[...][None]).reshape(RT, SEG)
        sbuf[:, pl.ds(at, SEG)] = sc
        best = jnp.max(jnp.maximum(mbuf[...], lane_max(sc)), axis=1, keepdims=True) * SCALE
        mbuf[...] = jnp.broadcast_to(best, (RT, HD))
        accbuf[...] = jnp.zeros((RT, KVW), jnp.float32)

        @pl.when(u < UNITS - 1)
        def _():
            relay_resp(u + 1)

        def weights(at, size):
            m = mbuf[...]
            m = jnp.concatenate([m] * (size // HD), axis=1)
            return jnp.exp2(sbuf[:, pl.ds(at, size)] * SCALE - m).astype(jnp.bfloat16)

        def add_prompt(t, _):
            at = pl.multiple_of(t * PCH, PCH)
            accbuf[...] += jnp.dot(weights(at, PCH), vp[pl.ds(at, PCH), :], preferred_element_type=jnp.float32)
            return 0

        lax.fori_loop(0, NPROMPT // PCH, add_prompt, 0)

        def add_resp(t, _):
            at = pl.multiple_of(NPROMPT + t * SEG, HD)
            vx = jnp.concatenate([resp_keys(t)[:, HD:], jnp.ones((SEG, HD), jnp.bfloat16)], axis=1)
            accbuf[...] += jnp.dot(weights(at, SEG), vx, preferred_element_type=jnp.float32)
            return 0

        lax.fori_loop(0, g + 1, add_resp, 0)
        acc = accbuf[...]
        res = (acc[:, :HD] / acc[:, HD:]).reshape(GROUP, NC * ROWS, HD)
        pos = lax.broadcasted_iota(jnp.int32, (NC * ROWS, HD), 0) + (g * SEG + z * (NC * ROWS))
        alive = pos < rlen[0, cand]
        for h in range(GROUP):
            piece = jnp.where(alive, res[h], 0.0).astype(jnp.bfloat16)
            obuf[cand, g, :, :, h * HD : (h + 1) * HD] = piece.reshape(NC, ROWS, HD)

    def o_ref(cand, index):
        return out.at[0, cand, :, pl.ds(pl.multiple_of(index * QW, QW), QW)]

    def o_remote(u, j):
        cand, g = u // NY, lax.rem(u, NY)
        return remote(
            obuf.at[cand, g, j], o_ref(cand, mine), o_s.at[u, j], o_r.at[cand, mine],
            (p, seq_of(g * NC + j, z)),
        )

    def o_local(u, j):
        cand, g = u // NY, lax.rem(u, NY)
        return pltpu.make_async_copy(obuf.at[cand, g, j], o_ref(cand, mine), o_r.at[cand, mine])

    def unit_step(u, _):
        cand, g = u // NY, lax.rem(u, NY)
        for j in range(NC):
            landed(qbuf.at[cand, g, j], q_r.at[cand, g * NC + j])
        wait_z(lambda zz: rbuf.at[cand, g, zz], lambda zz: zr_r.at[u, zz])
        attend(u)
        for j in range(NC):
            @pl.when(g * NC + j == mine)
            def _():
                o_local(u, j).start()

            @pl.when(g * NC + j != mine)
            def _():
                o_remote(u, j).start()
        return 0

    lax.fori_loop(0, UNITS, unit_step, 0)

    for k in range(1, NY * NC):
        for cand in range(2):
            q_copy(k, cand).wait_send()
        r_copy(k).wait_send()
        p_copy(k).wait_send()

    @pl.when(p != mine)
    def _():
        p_copy(0).wait_send()

    each_near(lambda slot, dz: zp_copy(z, dz, slot).wait_send(), True, True)

    @pl.when(middle)
    def _():
        zp_copy(far_src, far_dst, 4).wait_send()

    def end_step(u, _):
        each_near(lambda slot, dz: zr_copy(u, z, dz, slot).wait_send(), True, True)

        @pl.when(middle)
        def _():
            zr_copy(u, far_src, far_dst, 4).wait_send()

        for j in range(NC):
            @pl.when(lax.rem(u, NY) * NC + j != mine)
            def _():
                o_remote(u, j).wait_send()
        return 0

    lax.fori_loop(0, UNITS, end_step, 0)

    for cand in range(2):
        for k in range(NY * NC):
            landed(o_ref(cand, k), o_r.at[cand, k])


def shards(queries, resp_kv, prompt_kv, block_order, prompt_len, resp_len):
    bf16, f32 = jnp.bfloat16, jnp.float32
    dma = pltpu.SemaphoreType.DMA
    any_spec = pl.BlockSpec(memory_space=pl.ANY)
    smem = pl.BlockSpec(memory_space=pltpu.SMEM)
    return pl.pallas_call(
        kernel,
        out_shape=jax.ShapeDtypeStruct(queries.shape, bf16),
        in_specs=[any_spec] * 3 + [smem] * 3,
        out_specs=any_spec,
        scratch_shapes=[
            pltpu.VMEM((2, NY, NC, ROWS, QW), bf16),
            pltpu.VMEM((2, NY, NZ, NC, ROWS, KVW), bf16),
            pltpu.VMEM((NY, NZ, NC, CP, KVW), bf16),
            pltpu.VMEM((2, NY, NC, ROWS, QW), bf16),
            pltpu.VMEM((NPROMPT, HD), bf16),
            pltpu.VMEM((NPROMPT, KVW), bf16),
            pltpu.VMEM((RT, NPROMPT + NY * SEG), f32),
            pltpu.VMEM((RT, HD), f32),
            pltpu.VMEM((RT, KVW), f32),
            pltpu.VMEM((NC * ROWS, SEG), f32),
            dma((2, NY * NC)), dma((2, NY * NC)),
            dma((NY * NC,)), dma((NY * NC,)),
            dma((NP,)), dma((NY * NC,)),
            dma((5,)), dma((NZ,)),
            dma((UNITS, 5)), dma((UNITS, NZ)),
            dma((UNITS, NC)), dma((2, NY * NC)),
        ],
        compiler_params=pltpu.CompilerParams(
            collective_id=0, has_side_effects=True, vmem_limit_bytes=62 * 1024 * 1024
        ),
        name="attend",
    )(queries, resp_kv, prompt_kv, block_order, prompt_len, resp_len)


def solution(mesh):
    in_specs = (
        P("prompt", None, "seq", None),
        P("prompt", None, "seq", None),
        P(None, "seq", "prompt"),
        P("prompt", None),
        P("prompt"),
        P("prompt", None),
    )
    out_specs = P("prompt", None, "seq", None)
    return jax.shard_map(shards, mesh=mesh, in_specs=in_specs, out_specs=out_specs, check_vma=False)
```

```python
import functools
import math

import jax
import jax.numpy as jnp
from jax import lax
from jax.experimental import pallas as pl
from jax.experimental.pallas import tpu as pltpu
from jax.sharding import PartitionSpec as P

H = 64
KVH = 8
HD = 128
CP = 32
NP = 8
NY, NZ, NC = 4, 4, 2
ROWS = 48
GROUP = H // KVH
QW = GROUP * HD
KVW = 2 * HD
SEG = NZ * NC * ROWS
RT = GROUP * NC * ROWS
NPROMPT = NY * NZ * NC * CP
SCALE = math.log2(math.e) / math.sqrt(HD)
MESH = pl.DeviceIdType.MESH
NEG = -1e30
UNITS = 2 * NY
TILE = 4
TILES = GROUP // TILE
TW = TILE * HD
TR = TILE * NC * ROWS
AHEAD = 2


def kernel(
    q_in, r_in, p_in, order, plen, rlen, out,
    qbuf, rbuf, pbuf, obuf, kp, vp, sbuf, mbuf, accbuf, bias,
    q_s, q_r, r_s, r_r, p_s, p_r, zp_s, zp_r, zr_s, zr_r, o_s, o_r,
):
    p = lax.axis_index("prompt")
    s = lax.axis_index("seq")
    y = s // (NZ * NC)
    z = lax.rem(s, NZ * NC) // NC
    c = lax.rem(s, NC)
    mine = y * NC + c
    home = lax.div(p, NC) * (NZ * NC) + z * NC + lax.rem(p, NC)

    def seq_of(index, zz):
        return lax.div(index, NC) * (NZ * NC) + zz * NC + lax.rem(index, NC)

    def at_rel(k):
        return lax.rem(mine + k, NY * NC)

    def remote(src, dst, ss, rs, dev):
        return pltpu.make_async_remote_copy(
            src_ref=src, dst_ref=dst, send_sem=ss, recv_sem=rs, device_id=dev, device_id_type=MESH
        )

    def landed(ref, sem):
        pltpu.make_async_copy(ref, ref, sem).wait()

    barrier = pltpu.get_barrier_semaphore()

    def greet(dev):
        pl.semaphore_signal(barrier, inc=1, device_id=dev, device_id_type=MESH)

    for k in range(1, NY * NC):
        greet((p, seq_of(at_rel(k), z)))
    for k in range(1, NZ):
        greet((p, y * (NZ * NC) + lax.rem(z + k, NZ) * NC + c))
    for k in range(1, NP):
        greet((lax.rem(p + k, NP), home))
    for k in range(1, NY * NC):
        greet((mine, seq_of(at_rel(k), z)))

    @pl.when(p != mine)
    def _():
        greet((p, home))
        greet((mine, s))

    extra = jnp.where(p != mine, 2, 0)
    pl.semaphore_wait(barrier, (NY * NC - 1) * 2 + (NZ - 1) + (NP - 1) + extra)

    def r_copy(k):
        t = at_rel(k)
        src = r_in.at[0, :, :, pl.ds(pl.multiple_of(t * KVW, KVW), KVW)]
        dst = rbuf.at[:, y, z, c]
        if k == 0:
            return pltpu.make_async_copy(src, dst, r_r.at[mine])
        return remote(src, dst, r_s.at[k], r_r.at[mine], (p, seq_of(t, z)))

    def q_copy(k, cand):
        t = at_rel(k)
        src = q_in.at[0, cand, :, pl.ds(pl.multiple_of(t * QW, QW), QW)]
        dst = qbuf.at[cand, y, c]
        if k == 0:
            return pltpu.make_async_copy(src, dst, q_r.at[cand, mine])
        return remote(src, dst, q_s.at[cand, k], q_r.at[cand, mine], (p, seq_of(t, z)))

    def p_copy(k):
        t = lax.rem(p + k, NP)
        return remote(p_in.at[t], pbuf.at[y, z, c], p_s.at[k], p_r.at[mine], (t, home))

    def p_local():
        return pltpu.make_async_copy(p_in.at[p], pbuf.at[y, z, c], p_r.at[mine])

    r_copy(0).start()
    for k in (1, NY * NC - 1):
        @pl.when(at_rel(k) // NC == y)
        def _(k=k):
            r_copy(k).start()

    for k in range(1, NP):
        p_copy(k).start()

    @pl.when(p != mine)
    def _():
        p_copy(0).start()

    @pl.when(p == mine)
    def _():
        p_local().start()

    for k in range(1, NY * NC):
        @pl.when(at_rel(k) // NC != y)
        def _(k=k):
            r_copy(k).start()

    def z_dev(zz):
        return (p, y * (NZ * NC) + zz * NC + c)

    def zp_copy(src_z, dst_z, slot):
        ref = pbuf.at[:, src_z]
        return remote(ref, ref, zp_s.at[slot], zp_r.at[src_z], z_dev(dst_z))

    def zr_copy(u, src_z, dst_z, slot):
        ref = rbuf.at[u // NY, lax.rem(u, NY), src_z]
        return remote(ref, ref, zr_s.at[u, slot], zr_r.at[u, src_z], z_dev(dst_z))

    middle = jnp.logical_and(z > 0, z < NZ - 1)
    far_dst = (z - 1) * (NZ - 1)
    far_src = (NZ - 1) - far_dst

    def each_near(act, early, late):
        for slot, dz in enumerate((2, -2, 1, -1)):
            there = jnp.logical_and(z + dz >= 0, z + dz < NZ)
            held = jnp.logical_and(middle, z + dz == far_dst)
            want = there
            if not early:
                want = jnp.logical_and(there, held)
            if not late:
                want = jnp.logical_and(there, jnp.logical_not(held))

            @pl.when(want)
            def _(slot=slot, dz=dz):
                act(slot, z + dz)

    def send_unit(u, early, late):
        each_near(lambda slot, dz: zr_copy(u, z, dz, slot).start(), early, late)

    def start_q():
        for cand in range(2):
            for k in range(NY * NC):
                q_copy(k, cand).start()

    def unit_of(i):
        return i - 2 + jnp.where(i - 2 >= y, 1, 0)

    def relay_late(i):
        u = unit_of(i + AHEAD)
        send_unit(u, False, True)

    def relay_resp(i):
        u = unit_of(i)

        @pl.when(middle)
        def _():
            landed(rbuf.at[u // NY, lax.rem(u, NY), far_src], zr_r.at[u, far_src])
            zr_copy(u, far_src, far_dst, 4).start()

        @pl.when(i + AHEAD < UNITS + 1)
        def _():
            relay_late(i)

    for j in range(NC):
        landed(rbuf.at[:, y, z, j], r_r.at[y * NC + j])
    send_unit(y, True, True)
    start_q()
    for i in range(NY):
        for j in range(NC):
            landed(pbuf.at[i, z, j], p_r.at[i * NC + j])
    each_near(lambda slot, dz: zp_copy(z, dz, slot).start(), True, True)
    for i in range(NY):
        @pl.when(i != y)
        def _(i=i):
            for j in range(NC):
                landed(rbuf.at[:, i, z, j], r_r.at[i * NC + j])
    for u in range(UNITS):
        @pl.when(u != y)
        def _(u=u):
            send_unit(u, True, False)

    @pl.when(middle)
    def _():
        landed(rbuf.at[0, y, far_src], zr_r.at[y, far_src])
        zr_copy(y, far_src, far_dst, 4).start()

    relay_late(0)

    @pl.when(middle)
    def _():
        landed(pbuf.at[:, far_src], zp_r.at[far_src])
        zp_copy(far_src, far_dst, 4).start()

    relay_late(1)
    relay_resp(2)

    row_at = lax.broadcasted_iota(jnp.int32, (NC * ROWS, SEG), 0) + z * (NC * ROWS)
    col_at = lax.broadcasted_iota(jnp.int32, (NC * ROWS, SEG), 1)
    bias[...] = jnp.where(col_at <= row_at, 0.0, NEG)

    def wait_z(ref_of, sem_of):
        for k in range(1, NZ):
            src = lax.rem(z + k, NZ)
            relayed = jnp.logical_and(middle, src == far_src)

            @pl.when(jnp.logical_not(relayed))
            def _():
                landed(ref_of(src), sem_of(src))

    wait_z(lambda zz: pbuf.at[:, zz], lambda zz: zp_r.at[zz])

    positions = []
    for i in range(NY * NZ * NC):
        positions.append(order[0, i] * CP + lax.broadcasted_iota(jnp.int32, (CP, HD), 0))
    position = jnp.concatenate(positions, axis=0)
    live = position < plen[0]
    whole = pbuf[...].reshape(NPROMPT, KVW)
    keys = whole[:, :HD].astype(jnp.float32)
    vals = whole[:, HD:].astype(jnp.float32)
    first = jnp.sum(jnp.where(position == 0, keys, 0.0), axis=0, keepdims=True)
    kp[...] = jnp.where(live, keys, first).astype(jnp.bfloat16)
    vp[:, :HD] = jnp.where(live, vals, 0.0).astype(jnp.bfloat16)
    vp[:, HD:] = jnp.where(live, 1.0, 0.0).astype(jnp.bfloat16)

    def o_ref(cand, index, t):
        return out.at[0, cand, :, pl.ds(pl.multiple_of(index * QW + t * TW, TW), TW)]

    def o_remote(u, t, j):
        cand, g = u // NY, lax.rem(u, NY)
        return remote(
            obuf.at[cand, g, t, j], o_ref(cand, mine, t), o_s.at[u, t, j], o_r.at[cand, t, mine],
            (p, seq_of(g * NC + j, z)),
        )

    def o_local(u, t, j):
        cand, g = u // NY, lax.rem(u, NY)
        return pltpu.make_async_copy(obuf.at[cand, g, t, j], o_ref(cand, mine, t), o_r.at[cand, t, mine])

    def send_out(u, t):
        for j in range(NC):
            to = lax.rem(u, NY) * NC + j

            @pl.when(to == mine)
            def _(j=j):
                o_local(u, t, j).start()

            @pl.when(to != mine)
            def _(j=j):
                o_remote(u, t, j).start()

    dims = (((1,), (1,)), ((), ()))

    def lane_max(x):
        best = x[:, :HD]
        for t in range(1, x.shape[1] // HD):
            best = jnp.maximum(best, x[:, t * HD : (t + 1) * HD])
        return best

    def attend(u, g):
        cand = u // NY
        block = qbuf.at[cand, g]
        segments = [None] + list(range(g + 1))

        def span(seg):
            return (0, NPROMPT) if seg is None else (NPROMPT + seg * SEG, SEG)

        def rows_of(t):
            return pl.ds(t * TR, TR)

        def resp_rows(seg):
            return rbuf[cand, seg].reshape(SEG, KVW)

        def score(t, seg):
            q = block[:, :, t * TW : (t + 1) * TW]
            q = jnp.concatenate(
                [q[:, :, h * HD : (h + 1) * HD].reshape(NC * ROWS, HD) for h in range(TILE)], axis=0
            )
            at, size = span(seg)
            k = kp[...] if seg is None else resp_rows(seg)[:, :HD]
            sc = lax.dot_general(q, k, dims, preferred_element_type=jnp.float32)
            if seg == g:
                sc = (sc.reshape(TILE, NC * ROWS, SEG) + bias[...][None]).reshape(TR, SEG)
            sbuf[rows_of(t), pl.ds(at, size)] = sc
            best = lane_max(sc)
            if seg is not None:
                best = jnp.maximum(mbuf[rows_of(t)], best)
            if seg == g:
                best = jnp.broadcast_to(jnp.max(best, axis=1, keepdims=True) * SCALE, (TR, HD))
            mbuf[rows_of(t)] = best

        def add(t, seg):
            at, size = span(seg)
            m = jnp.concatenate([mbuf[rows_of(t)]] * (size // HD), axis=1)
            w = jnp.exp2(sbuf[rows_of(t), pl.ds(at, size)] * SCALE - m).astype(jnp.bfloat16)
            if seg is None:
                v = vp[...]
            else:
                v = jnp.concatenate([resp_rows(seg)[:, HD:], jnp.ones((SEG, HD), jnp.bfloat16)], axis=1)
            part = jnp.dot(w, v, preferred_element_type=jnp.float32)
            accbuf[rows_of(t)] = part if seg is None else accbuf[rows_of(t)] + part

        def finish(t):
            acc = accbuf[rows_of(t)]
            res = (acc[:, :HD] / acc[:, HD:]).reshape(TILE, NC * ROWS, HD)
            pos = lax.broadcasted_iota(jnp.int32, (NC * ROWS, HD), 0) + (g * SEG + z * (NC * ROWS))
            alive = pos < rlen[0, cand]
            for h in range(TILE):
                piece = jnp.where(alive, res[h], 0.0).astype(jnp.bfloat16)
                obuf[cand, g, t, :, :, h * HD : (h + 1) * HD] = piece.reshape(NC, ROWS, HD)
            send_out(u, t)

        for seg in segments:
            score(0, seg)

        @pl.when(u + 3 < UNITS + 1)
        def _():
            relay_resp(u + 3)

        for t in range(TILES):
            for seg in segments:
                if t + 1 < TILES:
                    score(t + 1, seg)
                add(t, seg)
            finish(t)

    def unit_step(u, _):
        cand, g = u // NY, lax.rem(u, NY)
        for j in range(NC):
            landed(qbuf.at[cand, g, j], q_r.at[cand, g * NC + j])
        wait_z(lambda zz: rbuf.at[cand, g, zz], lambda zz: zr_r.at[u, zz])
        for k in range(NY):
            @pl.when(g == k)
            def _(k=k):
                attend(u, k)
        return 0

    lax.fori_loop(0, UNITS, unit_step, 0)

    for k in range(1, NY * NC):
        for cand in range(2):
            q_copy(k, cand).wait_send()
        r_copy(k).wait_send()
        p_copy(k).wait_send()

    @pl.when(p != mine)
    def _():
        p_copy(0).wait_send()

    each_near(lambda slot, dz: zp_copy(z, dz, slot).wait_send(), True, True)

    @pl.when(middle)
    def _():
        zp_copy(far_src, far_dst, 4).wait_send()

    def end_step(u, _):
        each_near(lambda slot, dz: zr_copy(u, z, dz, slot).wait_send(), True, True)

        @pl.when(middle)
        def _():
            zr_copy(u, far_src, far_dst, 4).wait_send()

        for t in range(TILES):
            for j in range(NC):
                @pl.when(lax.rem(u, NY) * NC + j != mine)
                def _(t=t, j=j):
                    o_remote(u, t, j).wait_send()
        return 0

    lax.fori_loop(0, UNITS, end_step, 0)

    for cand in range(2):
        for t in range(TILES):
            for k in range(NY * NC):
                landed(o_ref(cand, k, t), o_r.at[cand, t, k])


def shards(queries, resp_kv, prompt_kv, block_order, prompt_len, resp_len):
    bf16, f32 = jnp.bfloat16, jnp.float32
    dma = pltpu.SemaphoreType.DMA
    any_spec = pl.BlockSpec(memory_space=pl.ANY)
    smem = pl.BlockSpec(memory_space=pltpu.SMEM)
    return pl.pallas_call(
        kernel,
        out_shape=jax.ShapeDtypeStruct(queries.shape, bf16),
        in_specs=[any_spec] * 3 + [smem] * 3,
        out_specs=any_spec,
        scratch_shapes=[
            pltpu.VMEM((2, NY, NC, ROWS, QW), bf16),
            pltpu.VMEM((2, NY, NZ, NC, ROWS, KVW), bf16),
            pltpu.VMEM((NY, NZ, NC, CP, KVW), bf16),
            pltpu.VMEM((2, NY, TILES, NC, ROWS, TW), bf16),
            pltpu.VMEM((NPROMPT, HD), bf16),
            pltpu.VMEM((NPROMPT, KVW), bf16),
            pltpu.VMEM((RT, NPROMPT + NY * SEG), f32),
            pltpu.VMEM((RT, HD), f32),
            pltpu.VMEM((RT, KVW), f32),
            pltpu.VMEM((NC * ROWS, SEG), f32),
            dma((2, NY * NC)), dma((2, NY * NC)),
            dma((NY * NC,)), dma((NY * NC,)),
            dma((NP,)), dma((NY * NC,)),
            dma((5,)), dma((NZ,)),
            dma((UNITS, 5)), dma((UNITS, NZ)),
            dma((UNITS, TILES, NC)), dma((2, TILES, NY * NC)),
        ],
        compiler_params=pltpu.CompilerParams(
            collective_id=0, has_side_effects=True, vmem_limit_bytes=62 * 1024 * 1024
        ),
        name="attend",
    )(queries, resp_kv, prompt_kv, block_order, prompt_len, resp_len)


def solution(mesh):
    in_specs = (
        P("prompt", None, "seq", None),
        P("prompt", None, "seq", None),
        P(None, "seq", "prompt"),
        P("prompt", None),
        P("prompt"),
        P("prompt", None),
    )
    out_specs = P("prompt", None, "seq", None)
    return jax.shard_map(shards, mesh=mesh, in_specs=in_specs, out_specs=out_specs, check_vma=False)
```

```python
import functools
import math

import jax
import jax.numpy as jnp
from jax import lax
from jax.experimental import pallas as pl
from jax.experimental.pallas import tpu as pltpu
from jax.sharding import PartitionSpec as P

H = 64
KVH = 8
HD = 128
CP = 32
NP = 8
NY, NZ, NC = 4, 4, 2
ROWS = 48
GROUP = H // KVH
QW = GROUP * HD
KVW = 2 * HD
SEG = NZ * NC * ROWS
RT = GROUP * NC * ROWS
NPROMPT = NY * NZ * NC * CP
SCALE = math.log2(math.e) / math.sqrt(HD)
MESH = pl.DeviceIdType.MESH
NEG = -1e30
UNITS = 2 * NY
TILE = 4
TILES = GROUP // TILE
TW = TILE * HD
TR = TILE * NC * ROWS
AHEAD = 2
EARLY = 1


def kernel(
    q_in, r_in, p_in, order, plen, rlen, out,
    qbuf, rbuf, pbuf, obuf, kp, vp, sbuf, mbuf, accbuf, bias,
    q_s, q_r, r_s, r_r, p_s, p_r, zp_s, zp_r, zr_s, zr_r, o_s, o_r,
):
    p = lax.axis_index("prompt")
    s = lax.axis_index("seq")
    y = s // (NZ * NC)
    z = lax.rem(s, NZ * NC) // NC
    c = lax.rem(s, NC)
    mine = y * NC + c
    home = lax.div(p, NC) * (NZ * NC) + z * NC + lax.rem(p, NC)

    def seq_of(index, zz):
        return lax.div(index, NC) * (NZ * NC) + zz * NC + lax.rem(index, NC)

    def at_rel(k):
        return lax.rem(mine + k, NY * NC)

    def remote(src, dst, ss, rs, dev):
        return pltpu.make_async_remote_copy(
            src_ref=src, dst_ref=dst, send_sem=ss, recv_sem=rs, device_id=dev, device_id_type=MESH
        )

    def landed(ref, sem):
        pltpu.make_async_copy(ref, ref, sem).wait()

    barrier = pltpu.get_barrier_semaphore()

    def greet(dev):
        pl.semaphore_signal(barrier, inc=1, device_id=dev, device_id_type=MESH)

    for k in range(1, NY * NC):
        greet((p, seq_of(at_rel(k), z)))
    for k in range(1, NZ):
        greet((p, y * (NZ * NC) + lax.rem(z + k, NZ) * NC + c))
    for k in range(1, NP):
        greet((lax.rem(p + k, NP), home))
    for k in range(1, NY * NC):
        greet((mine, seq_of(at_rel(k), z)))

    @pl.when(p != mine)
    def _():
        greet((p, home))
        greet((mine, s))


    def r_copy(k):
        t = at_rel(k)
        src = r_in.at[0, :, :, pl.ds(pl.multiple_of(t * KVW, KVW), KVW)]
        dst = rbuf.at[:, y, z, c]
        if k == 0:
            return pltpu.make_async_copy(src, dst, r_r.at[y])
        return remote(src, dst, r_s.at[0], r_r.at[y], (p, seq_of(t, z)))

    def q_copy(k, cand):
        t = at_rel(k)
        src = q_in.at[0, cand, :, pl.ds(pl.multiple_of(t * QW, QW), QW)]
        dst = qbuf.at[cand, mine]
        if k == 0:
            return pltpu.make_async_copy(src, dst, q_r.at[cand, y])
        return remote(src, dst, q_s.at[0], q_r.at[cand, y], (p, seq_of(t, z)))

    def p_copy(k):
        t = lax.rem(p + k, NP)
        return remote(p_in.at[t], pbuf.at[y, z, c], p_s.at[0], p_r.at[0], (t, home))

    def p_local():
        return pltpu.make_async_copy(p_in.at[p], pbuf.at[y, z, c], p_r.at[0])

    r_copy(0).start()
    for cand in range(2):
        q_copy(0, cand).start()

    row_at = lax.broadcasted_iota(jnp.int32, (NC * ROWS, SEG), 0) + z * (NC * ROWS)
    col_at = lax.broadcasted_iota(jnp.int32, (NC * ROWS, SEG), 1)
    bias[...] = jnp.where(col_at <= row_at, 0.0, NEG)

    extra = jnp.where(p != mine, 2, 0)
    pl.semaphore_wait(barrier, (NY * NC - 1) * 2 + (NZ - 1) + (NP - 1) + extra)

    for k in (1, NY * NC - 1):
        @pl.when(at_rel(k) // NC == y)
        def _(k=k):
            r_copy(k).start()

    for k in range(1, NP):
        p_copy(k).start()

    @pl.when(p != mine)
    def _():
        p_copy(0).start()

    @pl.when(p == mine)
    def _():
        p_local().start()

    for k in range(1, NY * NC):
        @pl.when(at_rel(k) // NC != y)
        def _(k=k):
            r_copy(k).start()

    def z_dev(zz):
        return (p, y * (NZ * NC) + zz * NC + c)

    def zp_copy(src_z, dst_z):
        ref = pbuf.at[:, src_z]
        return remote(ref, ref, zp_s.at[0], zp_r.at[src_z], z_dev(dst_z))

    def zr_copy(u, src_z, dst_z):
        ref = rbuf.at[u // NY, lax.rem(u, NY), src_z]
        return remote(ref, ref, zr_s.at[0], zr_r.at[u, src_z], z_dev(dst_z))

    middle = jnp.logical_and(z > 0, z < NZ - 1)
    far_dst = (z - 1) * (NZ - 1)
    far_src = (NZ - 1) - far_dst

    def each_near(act, early, late):
        for dz in (2, -2, 1, -1):
            there = jnp.logical_and(z + dz >= 0, z + dz < NZ)
            held = jnp.logical_and(middle, z + dz == far_dst)
            want = there
            if not early:
                want = jnp.logical_and(there, held)
            if not late:
                want = jnp.logical_and(there, jnp.logical_not(held))

            @pl.when(want)
            def _(dz=dz):
                act(z + dz)

    def send_unit(u, early, late):
        each_near(lambda zz: zr_copy(u, z, zz).start(), early, late)

    def start_q():
        for cand in range(2):
            for k in range(1, NY * NC):
                q_copy(k, cand).start()

    def unit_of(i):
        return i - 2 + jnp.where(i - 2 >= y, 1, 0)

    def relay_late(i):
        send_unit(unit_of(i + AHEAD), False, True)

    def relay_resp(i):
        u = unit_of(i)

        @pl.when(middle)
        def _():
            landed(rbuf.at[u // NY, lax.rem(u, NY), far_src], zr_r.at[u, far_src])
            zr_copy(u, far_src, far_dst).start()

        @pl.when(i + AHEAD < UNITS + 1)
        def _():
            relay_late(i)

    landed(rbuf.at[:, y, z], r_r.at[y])
    send_unit(y, True, True)
    start_q()
    landed(pbuf.at[:, z], p_r.at[0])
    each_near(lambda zz: zp_copy(z, zz).start(), True, True)
    for i in range(NY):
        @pl.when(i != y)
        def _(i=i):
            landed(rbuf.at[:, i, z], r_r.at[i])
    for u in range(UNITS):
        @pl.when(u != y)
        def _(u=u):
            send_unit(u, True, False)

    for i in range(2, AHEAD):
        send_unit(unit_of(i), False, True)

    @pl.when(middle)
    def _():
        landed(rbuf.at[0, y, far_src], zr_r.at[y, far_src])
        zr_copy(y, far_src, far_dst).start()

    relay_late(0)

    @pl.when(middle)
    def _():
        landed(pbuf.at[:, far_src], zp_r.at[far_src])
        zp_copy(far_src, far_dst).start()

    relay_late(1)

    for i in range(2, 3 + EARLY):
        relay_resp(i)

    def wait_z(ref_of, sem_of):
        for k in range(1, NZ):
            src = lax.rem(z + k, NZ)
            relayed = jnp.logical_and(middle, src == far_src)

            @pl.when(jnp.logical_not(relayed))
            def _():
                landed(ref_of(src), sem_of(src))

    wait_z(lambda zz: pbuf.at[:, zz], lambda zz: zp_r.at[zz])

    positions = []
    for i in range(NY * NZ * NC):
        positions.append(order[0, i] * CP + lax.broadcasted_iota(jnp.int32, (CP, HD), 0))
    position = jnp.concatenate(positions, axis=0)
    live = position < plen[0]
    whole = pbuf[...].reshape(NPROMPT, KVW)
    keys = whole[:, :HD].astype(jnp.float32)
    vals = whole[:, HD:].astype(jnp.float32)
    first = jnp.sum(jnp.where(position == 0, keys, 0.0), axis=0, keepdims=True)
    kp[...] = jnp.where(live, keys, first).astype(jnp.bfloat16)
    vp[:, :HD] = jnp.where(live, vals, 0.0).astype(jnp.bfloat16)
    vp[:, HD:] = jnp.where(live, 1.0, 0.0).astype(jnp.bfloat16)

    def o_ref(cand, index, t):
        return out.at[0, cand, :, pl.ds(pl.multiple_of(index * QW + t * TW, TW), TW)]

    def o_remote(u, t, j):
        cand, g = u // NY, lax.rem(u, NY)
        return remote(
            obuf.at[cand, t, g * NC + j], o_ref(cand, mine, t), o_s.at[0], o_r.at[0],
            (p, seq_of(g * NC + j, z)),
        )

    def o_local(u, t, j):
        cand, g = u // NY, lax.rem(u, NY)
        return pltpu.make_async_copy(obuf.at[cand, t, g * NC + j], o_ref(cand, mine, t), o_r.at[0])

    def send_out(u, t):
        for j in range(NC):
            to = lax.rem(u, NY) * NC + j

            @pl.when(to == mine)
            def _(j=j):
                o_local(u, t, j).start()

            @pl.when(to != mine)
            def _(j=j):
                o_remote(u, t, j).start()

    dims = (((1,), (1,)), ((), ()))

    def lane_max(x):
        best = x[:, :HD]
        for t in range(1, x.shape[1] // HD):
            best = jnp.maximum(best, x[:, t * HD : (t + 1) * HD])
        return best

    def attend(u, g):
        cand = u // NY
        block = qbuf.at[cand, pl.ds(g * NC, NC)]
        segments = [None] + list(range(g + 1))

        def span(seg):
            return (0, NPROMPT) if seg is None else (NPROMPT + seg * SEG, SEG)

        def rows_of(t):
            return pl.ds(t * TR, TR)

        def resp_rows(seg):
            return rbuf[cand, seg].reshape(SEG, KVW)

        def score(t, seg):
            q = block[:, :, t * TW : (t + 1) * TW]
            q = jnp.concatenate(
                [q[:, :, h * HD : (h + 1) * HD].reshape(NC * ROWS, HD) for h in range(TILE)], axis=0
            )
            at, size = span(seg)
            k = kp[...] if seg is None else resp_rows(seg)[:, :HD]
            sc = lax.dot_general(q, k, dims, preferred_element_type=jnp.float32)
            if seg == g:
                sc = (sc.reshape(TILE, NC * ROWS, SEG) + bias[...][None]).reshape(TR, SEG)
            sbuf[rows_of(t), pl.ds(at, size)] = sc
            best = lane_max(sc)
            if seg is not None:
                best = jnp.maximum(mbuf[rows_of(t)], best)
            if seg == g:
                best = jnp.broadcast_to(jnp.max(best, axis=1, keepdims=True) * SCALE, (TR, HD))
            mbuf[rows_of(t)] = best

        def add(t, seg):
            at, size = span(seg)
            m = jnp.concatenate([mbuf[rows_of(t)]] * (size // HD), axis=1)
            w = jnp.exp2(sbuf[rows_of(t), pl.ds(at, size)] * SCALE - m).astype(jnp.bfloat16)
            if seg is None:
                v = vp[...]
            else:
                v = jnp.concatenate([resp_rows(seg)[:, HD:], jnp.ones((SEG, HD), jnp.bfloat16)], axis=1)
            part = jnp.dot(w, v, preferred_element_type=jnp.float32)
            accbuf[rows_of(t)] = part if seg is None else accbuf[rows_of(t)] + part

        def finish(t):
            acc = accbuf[rows_of(t)]
            res = (acc[:, :HD] / acc[:, HD:]).reshape(TILE, NC * ROWS, HD)
            pos = lax.broadcasted_iota(jnp.int32, (NC * ROWS, HD), 0) + (g * SEG + z * (NC * ROWS))
            alive = pos < rlen[0, cand]
            for h in range(TILE):
                piece = jnp.where(alive, res[h], 0.0).astype(jnp.bfloat16)
                obuf[cand, t, g * NC : (g + 1) * NC, :, h * HD : (h + 1) * HD] = piece.reshape(NC, ROWS, HD)
            send_out(u, t)

        for seg in segments[:-1]:
            score(0, seg)

        wait_z(lambda zz: rbuf.at[cand, g, zz], lambda zz: zr_r.at[u, zz])
        score(0, g)

        for t in range(TILES):
            for seg in segments:
                if t + 1 < TILES:
                    score(t + 1, seg)
                add(t, seg)
            finish(t)

    def unit_step(u, _):
        cand, g = u // NY, lax.rem(u, NY)
        @pl.when(u + 3 + EARLY < UNITS + 1)
        def _():
            relay_resp(u + 3 + EARLY)

        landed(qbuf.at[cand, pl.ds(g * NC, NC)], q_r.at[cand, g])
        for k in range(NY):
            @pl.when(g == k)
            def _(k=k):
                attend(u, k)
        return 0

    lax.fori_loop(0, UNITS, unit_step, 0)

    most = NY * NC - 1
    landed(qbuf.at[:, pl.ds(0, most)], q_s.at[0])
    landed(r_in.at[0, :, :, pl.ds(0, most * KVW)], r_s.at[0])

    @pl.when(p != mine)
    def _():
        landed(p_in, p_s.at[0])

    @pl.when(p == mine)
    def _():
        landed(p_in.at[pl.ds(0, NP - 1)], p_s.at[0])

    @pl.when(middle)
    def _():
        landed(pbuf, zp_s.at[0])
        landed(rbuf, zr_s.at[0])

    @pl.when(jnp.logical_not(middle))
    def _():
        landed(pbuf.at[:, pl.ds(0, 2)], zp_s.at[0])
        landed(rbuf.at[:, :, pl.ds(0, 2)], zr_s.at[0])

    landed(obuf.at[:, :, pl.ds(0, most)], o_s.at[0])
    landed(out, o_r.at[0])


def shards(queries, resp_kv, prompt_kv, block_order, prompt_len, resp_len):
    bf16, f32 = jnp.bfloat16, jnp.float32
    dma = pltpu.SemaphoreType.DMA
    any_spec = pl.BlockSpec(memory_space=pl.ANY)
    smem = pl.BlockSpec(memory_space=pltpu.SMEM)
    return pl.pallas_call(
        kernel,
        out_shape=jax.ShapeDtypeStruct(queries.shape, bf16),
        in_specs=[any_spec] * 3 + [smem] * 3,
        out_specs=any_spec,
        scratch_shapes=[
            pltpu.VMEM((2, NY * NC, ROWS, QW), bf16),
            pltpu.VMEM((2, NY, NZ, NC, ROWS, KVW), bf16),
            pltpu.VMEM((NY, NZ, NC, CP, KVW), bf16),
            pltpu.VMEM((2, TILES, NY * NC, ROWS, TW), bf16),
            pltpu.VMEM((NPROMPT, HD), bf16),
            pltpu.VMEM((NPROMPT, KVW), bf16),
            pltpu.VMEM((RT, NPROMPT + NY * SEG), f32),
            pltpu.VMEM((RT, HD), f32),
            pltpu.VMEM((RT, KVW), f32),
            pltpu.VMEM((NC * ROWS, SEG), f32),
            dma((1,)), dma((2, NY)),
            dma((1,)), dma((NY,)),
            dma((1,)), dma((1,)),
            dma((1,)), dma((NZ,)),
            dma((1,)), dma((UNITS, NZ)),
            dma((1,)), dma((1,)),
        ],
        compiler_params=pltpu.CompilerParams(
            collective_id=0, has_side_effects=True, vmem_limit_bytes=62 * 1024 * 1024
        ),
        name="attend",
    )(queries, resp_kv, prompt_kv, block_order, prompt_len, resp_len)


def solution(mesh):
    in_specs = (
        P("prompt", None, "seq", None),
        P("prompt", None, "seq", None),
        P(None, "seq", "prompt"),
        P("prompt", None),
        P("prompt"),
        P("prompt", None),
    )
    out_specs = P("prompt", None, "seq", None)
    return jax.shard_map(shards, mesh=mesh, in_specs=in_specs, out_specs=out_specs, check_vma=False)
```

```python
import functools
import math

import jax
import jax.numpy as jnp
from jax import lax
from jax.experimental import pallas as pl
from jax.experimental.pallas import tpu as pltpu
from jax.sharding import PartitionSpec as P

H = 64
KVH = 8
HD = 128
CP = 32
NP = 8
NY, NZ, NC = 4, 4, 2
ROWS = 48
GROUP = H // KVH
QW = GROUP * HD
KVW = 2 * HD
SEG = NZ * NC * ROWS
RT = GROUP * NC * ROWS
NPROMPT = NY * NZ * NC * CP
SCALE = math.log2(math.e) / math.sqrt(HD)
MESH = pl.DeviceIdType.MESH
NEG = -1e30
UNITS = 2 * NY
TILE = 4
TILES = GROUP // TILE
TW = TILE * HD
TR = TILE * NC * ROWS
AHEAD = 2
EARLY = 1


def kernel(
    q_in, r_in, p_in, order, plen, rlen, out,
    qbuf, rbuf, pbuf, obuf, kp, vp, sbuf, mbuf, accbuf, bias,
    q_s, q_r, r_s, r_r, p_s, p_r, zp_s, zp_r, zr_s, zr_r, o_s, o_r,
):
    p = lax.axis_index("prompt")
    s = lax.axis_index("seq")
    y = s // (NZ * NC)
    z = lax.rem(s, NZ * NC) // NC
    c = lax.rem(s, NC)
    mine = y * NC + c
    home = lax.div(p, NC) * (NZ * NC) + z * NC + lax.rem(p, NC)

    def seq_of(index, zz):
        return lax.div(index, NC) * (NZ * NC) + zz * NC + lax.rem(index, NC)

    def at_rel(k):
        return lax.rem(mine + k, NY * NC)

    def remote(src, dst, ss, rs, dev):
        return pltpu.make_async_remote_copy(
            src_ref=src, dst_ref=dst, send_sem=ss, recv_sem=rs, device_id=dev, device_id_type=MESH
        )

    def landed(ref, sem):
        pltpu.make_async_copy(ref, ref, sem).wait()

    barrier = pltpu.get_barrier_semaphore()

    def greet(dev):
        pl.semaphore_signal(barrier, inc=1, device_id=dev, device_id_type=MESH)

    for k in range(1, NY * NC):
        greet((p, seq_of(at_rel(k), z)))
    for k in range(1, NZ):
        greet((p, y * (NZ * NC) + lax.rem(z + k, NZ) * NC + c))
    for k in range(1, NP):
        greet((lax.rem(p + k, NP), home))
    for k in range(1, NY * NC):
        greet((mine, seq_of(at_rel(k), z)))

    @pl.when(p != mine)
    def _():
        greet((p, home))
        greet((mine, s))


    def r_copy(k):
        t = at_rel(k)
        src = r_in.at[0, :, :, pl.ds(pl.multiple_of(t * KVW, KVW), KVW)]
        dst = rbuf.at[:, y, z, c]
        if k == 0:
            return pltpu.make_async_copy(src, dst, r_r.at[y])
        return remote(src, dst, r_s.at[0], r_r.at[y], (p, seq_of(t, z)))

    def q_copy(k, cand):
        t = at_rel(k)
        src = q_in.at[0, cand, :, pl.ds(pl.multiple_of(t * QW, QW), QW)]
        dst = qbuf.at[cand, mine]
        if k == 0:
            return pltpu.make_async_copy(src, dst, q_r.at[cand, y])
        return remote(src, dst, q_s.at[0], q_r.at[cand, y], (p, seq_of(t, z)))

    def p_copy(k):
        t = lax.rem(p + k, NP)
        return remote(p_in.at[t], pbuf.at[y, z, c], p_s.at[0], p_r.at[0], (t, home))

    def p_local():
        return pltpu.make_async_copy(p_in.at[p], pbuf.at[y, z, c], p_r.at[0])

    r_copy(0).start()
    for cand in range(2):
        q_copy(0, cand).start()

    for zz in range(1, NZ):
        @pl.when(zz > z)
        def _(zz=zz):
            rbuf[:, NY - 1, zz] = jnp.zeros((2, NC, ROWS, KVW), jnp.bfloat16)

    row_at = lax.broadcasted_iota(jnp.int32, (NC * ROWS, SEG), 0) + z * (NC * ROWS)
    col_at = lax.broadcasted_iota(jnp.int32, (NC * ROWS, SEG), 1)
    bias[...] = jnp.where(col_at <= row_at, 0.0, NEG)

    extra = jnp.where(p != mine, 2, 0)
    pl.semaphore_wait(barrier, (NY * NC - 1) * 2 + (NZ - 1) + (NP - 1) + extra)

    for k in (1, NY * NC - 1):
        @pl.when(at_rel(k) // NC == y)
        def _(k=k):
            r_copy(k).start()

    for k in range(1, NP):
        p_copy(k).start()

    @pl.when(p != mine)
    def _():
        p_copy(0).start()

    @pl.when(p == mine)
    def _():
        p_local().start()

    for k in range(1, NY * NC):
        @pl.when(at_rel(k) // NC != y)
        def _(k=k):
            r_copy(k).start()

    def z_dev(zz):
        return (p, y * (NZ * NC) + zz * NC + c)

    def zp_copy(src_z, dst_z):
        ref = pbuf.at[:, src_z]
        return remote(ref, ref, zp_s.at[0], zp_r.at[src_z], z_dev(dst_z))

    def zr_copy(u, src_z, dst_z):
        ref = rbuf.at[u // NY, lax.rem(u, NY), src_z]
        return remote(ref, ref, zr_s.at[0], zr_r.at[u, src_z], z_dev(dst_z))

    middle = jnp.logical_and(z > 0, z < NZ - 1)

    def relays(u):
        return jnp.logical_and(middle, jnp.logical_or(lax.rem(u, NY) < NY - 1, z == NZ - 2))

    far_dst = (z - 1) * (NZ - 1)
    far_src = (NZ - 1) - far_dst

    def each_near(act, early, late, last=False):
        for dz in (2, -2, 1, -1):
            there = jnp.logical_and(z + dz >= 0, z + dz < NZ)
            if dz < 0:
                there = jnp.logical_and(there, jnp.logical_not(last))
            held = jnp.logical_and(middle, z + dz == far_dst)
            want = there
            if not early:
                want = jnp.logical_and(there, held)
            if not late:
                want = jnp.logical_and(there, jnp.logical_not(held))

            @pl.when(want)
            def _(dz=dz):
                act(z + dz)

    def send_unit(u, early, late):
        each_near(lambda zz: zr_copy(u, z, zz).start(), early, late, lax.rem(u, NY) == NY - 1)

    def start_q():
        for cand in range(2):
            for k in range(1, NY * NC):
                q_copy(k, cand).start()

    def unit_of(i):
        return i - 2 + jnp.where(i - 2 >= y, 1, 0)

    def relay_late(i):
        send_unit(unit_of(i + AHEAD), False, True)

    def relay_resp(i):
        u = unit_of(i)

        @pl.when(relays(u))
        def _():
            landed(rbuf.at[u // NY, lax.rem(u, NY), far_src], zr_r.at[u, far_src])
            zr_copy(u, far_src, far_dst).start()

        @pl.when(i + AHEAD < UNITS + 1)
        def _():
            relay_late(i)

    landed(rbuf.at[:, y, z], r_r.at[y])
    send_unit(y, True, True)
    start_q()
    landed(pbuf.at[:, z], p_r.at[0])
    each_near(lambda zz: zp_copy(z, zz).start(), True, True)
    for i in range(NY):
        @pl.when(i != y)
        def _(i=i):
            landed(rbuf.at[:, i, z], r_r.at[i])
    for u in range(UNITS):
        @pl.when(u != y)
        def _(u=u):
            send_unit(u, True, False)

    for i in range(2, AHEAD):
        send_unit(unit_of(i), False, True)

    @pl.when(relays(y))
    def _():
        landed(rbuf.at[0, y, far_src], zr_r.at[y, far_src])
        zr_copy(y, far_src, far_dst).start()

    relay_late(0)

    @pl.when(middle)
    def _():
        landed(pbuf.at[:, far_src], zp_r.at[far_src])
        zp_copy(far_src, far_dst).start()

    relay_late(1)

    for i in range(2, 3 + EARLY):
        relay_resp(i)

    def wait_z(ref_of, sem_of, last=False):
        for k in range(1, NZ):
            src = lax.rem(z + k, NZ)
            relayed = jnp.logical_and(middle, src == far_src)

            @pl.when(jnp.logical_and(jnp.logical_not(relayed), src < z) if last else jnp.logical_not(relayed))
            def _():
                landed(ref_of(src), sem_of(src))

    wait_z(lambda zz: pbuf.at[:, zz], lambda zz: zp_r.at[zz])

    positions = []
    for i in range(NY * NZ * NC):
        positions.append(order[0, i] * CP + lax.broadcasted_iota(jnp.int32, (CP, HD), 0))
    position = jnp.concatenate(positions, axis=0)
    live = position < plen[0]
    whole = pbuf[...].reshape(NPROMPT, KVW)
    keys = whole[:, :HD].astype(jnp.float32)
    vals = whole[:, HD:].astype(jnp.float32)
    first = jnp.sum(jnp.where(position == 0, keys, 0.0), axis=0, keepdims=True)
    kp[...] = jnp.where(live, keys, first).astype(jnp.bfloat16)
    vp[:, :HD] = jnp.where(live, vals, 0.0).astype(jnp.bfloat16)
    vp[:, HD:] = jnp.where(live, 1.0, 0.0).astype(jnp.bfloat16)

    def o_ref(cand, index, t):
        return out.at[0, cand, :, pl.ds(pl.multiple_of(index * QW + t * TW, TW), TW)]

    def o_remote(u, t, j):
        cand, g = u // NY, lax.rem(u, NY)
        return remote(
            obuf.at[cand, t, g * NC + j], o_ref(cand, mine, t), o_s.at[0], o_r.at[0],
            (p, seq_of(g * NC + j, z)),
        )

    def o_local(u, t, j):
        cand, g = u // NY, lax.rem(u, NY)
        return pltpu.make_async_copy(obuf.at[cand, t, g * NC + j], o_ref(cand, mine, t), o_r.at[0])

    def send_out(u, t):
        for j in range(NC):
            to = lax.rem(u, NY) * NC + j

            @pl.when(to == mine)
            def _(j=j):
                o_local(u, t, j).start()

            @pl.when(to != mine)
            def _(j=j):
                o_remote(u, t, j).start()

    dims = (((1,), (1,)), ((), ()))

    def lane_max(x):
        best = x[:, :HD]
        for t in range(1, x.shape[1] // HD):
            best = jnp.maximum(best, x[:, t * HD : (t + 1) * HD])
        return best

    def attend(u, g):
        cand = u // NY
        block = qbuf.at[cand, pl.ds(g * NC, NC)]
        segments = [None] + list(range(g + 1))

        def span(seg):
            return (0, NPROMPT) if seg is None else (NPROMPT + seg * SEG, SEG)

        def rows_of(t):
            return pl.ds(t * TR, TR)

        def resp_rows(seg):
            return rbuf[cand, seg].reshape(SEG, KVW)

        def score(t, seg):
            q = block[:, :, t * TW : (t + 1) * TW]
            q = jnp.concatenate(
                [q[:, :, h * HD : (h + 1) * HD].reshape(NC * ROWS, HD) for h in range(TILE)], axis=0
            )
            at, size = span(seg)
            k = kp[...] if seg is None else resp_rows(seg)[:, :HD]
            sc = lax.dot_general(q, k, dims, preferred_element_type=jnp.float32)
            if seg == g:
                sc = (sc.reshape(TILE, NC * ROWS, SEG) + bias[...][None]).reshape(TR, SEG)
            sbuf[rows_of(t), pl.ds(at, size)] = sc
            best = lane_max(sc)
            if seg is not None:
                best = jnp.maximum(mbuf[rows_of(t)], best)
            if seg == g:
                best = jnp.broadcast_to(jnp.max(best, axis=1, keepdims=True) * SCALE, (TR, HD))
            mbuf[rows_of(t)] = best

        def add(t, seg):
            at, size = span(seg)
            m = jnp.concatenate([mbuf[rows_of(t)]] * (size // HD), axis=1)
            w = jnp.exp2(sbuf[rows_of(t), pl.ds(at, size)] * SCALE - m).astype(jnp.bfloat16)
            if seg is None:
                v = vp[...]
            else:
                v = jnp.concatenate([resp_rows(seg)[:, HD:], jnp.ones((SEG, HD), jnp.bfloat16)], axis=1)
            part = jnp.dot(w, v, preferred_element_type=jnp.float32)
            accbuf[rows_of(t)] = part if seg is None else accbuf[rows_of(t)] + part

        def finish(t):
            acc = accbuf[rows_of(t)]
            res = (acc[:, :HD] / acc[:, HD:]).reshape(TILE, NC * ROWS, HD)
            pos = lax.broadcasted_iota(jnp.int32, (NC * ROWS, HD), 0) + (g * SEG + z * (NC * ROWS))
            alive = pos < rlen[0, cand]
            for h in range(TILE):
                piece = jnp.where(alive, res[h], 0.0).astype(jnp.bfloat16)
                obuf[cand, t, g * NC : (g + 1) * NC, :, h * HD : (h + 1) * HD] = piece.reshape(NC, ROWS, HD)
            send_out(u, t)

        for seg in segments[:-1]:
            score(0, seg)

        wait_z(lambda zz: rbuf.at[cand, g, zz], lambda zz: zr_r.at[u, zz], g == NY - 1)
        score(0, g)

        for t in range(TILES):
            for seg in segments:
                if t + 1 < TILES:
                    score(t + 1, seg)
                add(t, seg)
            finish(t)

    def unit_step(u, _):
        cand, g = u // NY, lax.rem(u, NY)
        @pl.when(u + 3 + EARLY < UNITS + 1)
        def _():
            relay_resp(u + 3 + EARLY)

        landed(qbuf.at[cand, pl.ds(g * NC, NC)], q_r.at[cand, g])
        for k in range(NY):
            @pl.when(g == k)
            def _(k=k):
                attend(u, k)
        return 0

    lax.fori_loop(0, UNITS, unit_step, 0)

    most = NY * NC - 1
    landed(qbuf.at[:, pl.ds(0, most)], q_s.at[0])
    landed(r_in.at[0, :, :, pl.ds(0, most * KVW)], r_s.at[0])

    @pl.when(p != mine)
    def _():
        landed(p_in, p_s.at[0])

    @pl.when(p == mine)
    def _():
        landed(p_in.at[pl.ds(0, NP - 1)], p_s.at[0])

    @pl.when(middle)
    def _():
        landed(pbuf, zp_s.at[0])
        landed(qbuf.at[:, pl.ds(0, 7)], zr_s.at[0])

    @pl.when(jnp.logical_not(middle))
    def _():
        landed(pbuf.at[:, pl.ds(0, 2)], zp_s.at[0])

    @pl.when(z == 0)
    def _():
        landed(qbuf.at[:, pl.ds(0, 4)], zr_s.at[0])

    @pl.when(z == NZ - 1)
    def _():
        landed(qbuf.at[:, pl.ds(0, 3)], zr_s.at[0])

    landed(obuf.at[:, :, pl.ds(0, most)], o_s.at[0])
    landed(out, o_r.at[0])


def shards(queries, resp_kv, prompt_kv, block_order, prompt_len, resp_len):
    bf16, f32 = jnp.bfloat16, jnp.float32
    dma = pltpu.SemaphoreType.DMA
    any_spec = pl.BlockSpec(memory_space=pl.ANY)
    smem = pl.BlockSpec(memory_space=pltpu.SMEM)
    return pl.pallas_call(
        kernel,
        out_shape=jax.ShapeDtypeStruct(queries.shape, bf16),
        in_specs=[any_spec] * 3 + [smem] * 3,
        out_specs=any_spec,
        scratch_shapes=[
            pltpu.VMEM((2, NY * NC, ROWS, QW), bf16),
            pltpu.VMEM((2, NY, NZ, NC, ROWS, KVW), bf16),
            pltpu.VMEM((NY, NZ, NC, CP, KVW), bf16),
            pltpu.VMEM((2, TILES, NY * NC, ROWS, TW), bf16),
            pltpu.VMEM((NPROMPT, HD), bf16),
            pltpu.VMEM((NPROMPT, KVW), bf16),
            pltpu.VMEM((RT, NPROMPT + NY * SEG), f32),
            pltpu.VMEM((RT, HD), f32),
            pltpu.VMEM((RT, KVW), f32),
            pltpu.VMEM((NC * ROWS, SEG), f32),
            dma((1,)), dma((2, NY)),
            dma((1,)), dma((NY,)),
            dma((1,)), dma((1,)),
            dma((1,)), dma((NZ,)),
            dma((1,)), dma((UNITS, NZ)),
            dma((1,)), dma((1,)),
        ],
        compiler_params=pltpu.CompilerParams(
            collective_id=0, has_side_effects=True, vmem_limit_bytes=62 * 1024 * 1024
        ),
        name="attend",
    )(queries, resp_kv, prompt_kv, block_order, prompt_len, resp_len)


def solution(mesh):
    in_specs = (
        P("prompt", None, "seq", None),
        P("prompt", None, "seq", None),
        P(None, "seq", "prompt"),
        P("prompt", None),
        P("prompt"),
        P("prompt", None),
    )
    out_specs = P("prompt", None, "seq", None)
    return jax.shard_map(shards, mesh=mesh, in_specs=in_specs, out_specs=out_specs, check_vma=False)
```

```python
import functools
import math

import jax
import jax.numpy as jnp
from jax import lax
from jax.experimental import pallas as pl
from jax.experimental.pallas import tpu as pltpu
from jax.sharding import PartitionSpec as P

H = 64
KVH = 8
HD = 128
CP = 32
NP = 8
NY, NZ, NC = 4, 4, 2
ROWS = 48
GROUP = H // KVH
QW = GROUP * HD
KVW = 2 * HD
SEG = NZ * NC * ROWS
RT = GROUP * NC * ROWS
NPROMPT = NY * NZ * NC * CP
SCALE = math.log2(math.e) / math.sqrt(HD)
MESH = pl.DeviceIdType.MESH
NEG = -1e30
TOP = 3.4e38
UNITS = 2 * NY
TILE = 4
TILES = GROUP // TILE
TW = TILE * HD
TR = TILE * NC * ROWS
AHEAD = 2
EARLY = 1


def kernel(
    q_in, r_in, p_in, order, plen, rlen, out,
    qbuf, rbuf, pbuf, obuf, kp, vp, sbuf, mbuf, accbuf, bound,
    q_s, q_r, r_s, r_r, p_s, p_r, zp_s, zp_r, zr_s, zr_r, o_s, o_r,
):
    p = lax.axis_index("prompt")
    s = lax.axis_index("seq")
    y = s // (NZ * NC)
    z = lax.rem(s, NZ * NC) // NC
    c = lax.rem(s, NC)
    mine = y * NC + c
    home = lax.div(p, NC) * (NZ * NC) + z * NC + lax.rem(p, NC)

    def seq_of(index, zz):
        return lax.div(index, NC) * (NZ * NC) + zz * NC + lax.rem(index, NC)

    def at_rel(k):
        return lax.rem(mine + k, NY * NC)

    def remote(src, dst, ss, rs, dev):
        return pltpu.make_async_remote_copy(
            src_ref=src, dst_ref=dst, send_sem=ss, recv_sem=rs, device_id=dev, device_id_type=MESH
        )

    def landed(ref, sem):
        pltpu.make_async_copy(ref, ref, sem).wait()

    barrier = pltpu.get_barrier_semaphore()

    def greet(dev):
        pl.semaphore_signal(barrier, inc=1, device_id=dev, device_id_type=MESH)

    for k in range(1, NY * NC):
        greet((p, seq_of(at_rel(k), z)))
    for k in range(1, NZ):
        greet((p, y * (NZ * NC) + lax.rem(z + k, NZ) * NC + c))
    for k in range(1, NP):
        greet((lax.rem(p + k, NP), home))
    for k in range(1, NY * NC):
        greet((mine, seq_of(at_rel(k), z)))

    @pl.when(p != mine)
    def _():
        greet((p, home))
        greet((mine, s))


    def r_copy(k):
        t = at_rel(k)
        src = r_in.at[0, :, :, pl.ds(pl.multiple_of(t * KVW, KVW), KVW)]
        dst = rbuf.at[:, y, z, c]
        if k == 0:
            return pltpu.make_async_copy(src, dst, r_r.at[y])
        return remote(src, dst, r_s.at[0], r_r.at[y], (p, seq_of(t, z)))

    def q_copy(k, cand):
        t = at_rel(k)
        src = q_in.at[0, cand, :, pl.ds(pl.multiple_of(t * QW, QW), QW)]
        dst = qbuf.at[cand, mine]
        if k == 0:
            return pltpu.make_async_copy(src, dst, q_r.at[cand, y])
        return remote(src, dst, q_s.at[0], q_r.at[cand, y], (p, seq_of(t, z)))

    def p_copy(k):
        t = lax.rem(p + k, NP)
        return remote(p_in.at[t], pbuf.at[y, z, c], p_s.at[0], p_r.at[0], (t, home))

    def p_local():
        return pltpu.make_async_copy(p_in.at[p], pbuf.at[y, z, c], p_r.at[0])

    r_copy(0).start()
    for cand in range(2):
        q_copy(0, cand).start()

    for zz in range(1, NZ):
        @pl.when(zz > z)
        def _(zz=zz):
            rbuf[:, NY - 1, zz] = jnp.zeros((2, NC, ROWS, KVW), jnp.bfloat16)

    row_at = lax.broadcasted_iota(jnp.int32, (NC * ROWS, SEG), 0) + z * (NC * ROWS)
    col_at = lax.broadcasted_iota(jnp.int32, (NC * ROWS, SEG), 1)
    bound[...] = jnp.where(col_at <= row_at, TOP, NEG)

    extra = jnp.where(p != mine, 2, 0)
    pl.semaphore_wait(barrier, (NY * NC - 1) * 2 + (NZ - 1) + (NP - 1) + extra)

    for k in (1, NY * NC - 1):
        @pl.when(at_rel(k) // NC == y)
        def _(k=k):
            r_copy(k).start()

    for k in range(1, NP):
        p_copy(k).start()

    @pl.when(p != mine)
    def _():
        p_copy(0).start()

    @pl.when(p == mine)
    def _():
        p_local().start()

    for k in range(1, NY * NC):
        @pl.when(at_rel(k) // NC != y)
        def _(k=k):
            r_copy(k).start()

    def z_dev(zz):
        return (p, y * (NZ * NC) + zz * NC + c)

    def zp_copy(src_z, dst_z):
        ref = pbuf.at[:, src_z]
        return remote(ref, ref, zp_s.at[0], zp_r.at[src_z], z_dev(dst_z))

    def zr_copy(u, src_z, dst_z):
        ref = rbuf.at[u // NY, lax.rem(u, NY), src_z]
        return remote(ref, ref, zr_s.at[0], zr_r.at[u, src_z], z_dev(dst_z))

    middle = jnp.logical_and(z > 0, z < NZ - 1)

    def relays(u):
        return jnp.logical_and(middle, jnp.logical_or(lax.rem(u, NY) < NY - 1, z == NZ - 2))

    far_dst = (z - 1) * (NZ - 1)
    far_src = (NZ - 1) - far_dst

    def each_near(act, early, late, last=False):
        for dz in (2, -2, 1, -1):
            there = jnp.logical_and(z + dz >= 0, z + dz < NZ)
            if dz < 0:
                there = jnp.logical_and(there, jnp.logical_not(last))
            held = jnp.logical_and(middle, z + dz == far_dst)
            want = there
            if not early:
                want = jnp.logical_and(there, held)
            if not late:
                want = jnp.logical_and(there, jnp.logical_not(held))

            @pl.when(want)
            def _(dz=dz):
                act(z + dz)

    def send_unit(u, early, late):
        each_near(lambda zz: zr_copy(u, z, zz).start(), early, late, lax.rem(u, NY) == NY - 1)

    def start_q():
        for cand in range(2):
            for k in range(1, NY * NC):
                q_copy(k, cand).start()

    def unit_of(i):
        return i - 2 + jnp.where(i - 2 >= y, 1, 0)

    def relay_late(i):
        send_unit(unit_of(i + AHEAD), False, True)

    def relay_resp(i):
        u = unit_of(i)

        @pl.when(relays(u))
        def _():
            landed(rbuf.at[u // NY, lax.rem(u, NY), far_src], zr_r.at[u, far_src])
            zr_copy(u, far_src, far_dst).start()

        @pl.when(i + AHEAD < UNITS + 1)
        def _():
            relay_late(i)

    landed(rbuf.at[:, y, z], r_r.at[y])
    send_unit(y, True, True)
    start_q()
    landed(pbuf.at[:, z], p_r.at[0])
    each_near(lambda zz: zp_copy(z, zz).start(), True, True)
    for i in range(NY):
        @pl.when(i != y)
        def _(i=i):
            landed(rbuf.at[:, i, z], r_r.at[i])
    for u in range(UNITS):
        @pl.when(u != y)
        def _(u=u):
            send_unit(u, True, False)

    for i in range(2, AHEAD):
        send_unit(unit_of(i), False, True)

    @pl.when(relays(y))
    def _():
        landed(rbuf.at[0, y, far_src], zr_r.at[y, far_src])
        zr_copy(y, far_src, far_dst).start()

    relay_late(0)

    @pl.when(middle)
    def _():
        landed(pbuf.at[:, far_src], zp_r.at[far_src])
        zp_copy(far_src, far_dst).start()

    relay_late(1)

    for i in range(2, 3 + EARLY):
        relay_resp(i)

    def wait_z(ref_of, sem_of, last=False):
        for k in range(1, NZ):
            src = lax.rem(z + k, NZ)
            relayed = jnp.logical_and(middle, src == far_src)

            @pl.when(jnp.logical_and(jnp.logical_not(relayed), src < z) if last else jnp.logical_not(relayed))
            def _():
                landed(ref_of(src), sem_of(src))

    wait_z(lambda zz: pbuf.at[:, zz], lambda zz: zp_r.at[zz])

    positions = []
    for i in range(NY * NZ * NC):
        positions.append(order[0, i] * CP + lax.broadcasted_iota(jnp.int32, (CP, HD), 0))
    position = jnp.concatenate(positions, axis=0)
    live = position < plen[0]
    whole = pbuf[...].reshape(NPROMPT, KVW)
    keys = whole[:, :HD].astype(jnp.float32)
    vals = whole[:, HD:].astype(jnp.float32)
    first = jnp.sum(jnp.where(position == 0, keys, 0.0), axis=0, keepdims=True)
    kp[...] = jnp.where(live, keys, first).astype(jnp.bfloat16)
    vp[:, :HD] = jnp.where(live, vals, 0.0).astype(jnp.bfloat16)
    vp[:, HD:] = jnp.where(live, 1.0, 0.0).astype(jnp.bfloat16)

    def o_ref(cand, index, t):
        return out.at[0, cand, :, pl.ds(pl.multiple_of(index * QW + t * TW, TW), TW)]

    def o_remote(u, t, j):
        cand, g = u // NY, lax.rem(u, NY)
        return remote(
            obuf.at[cand, t, g * NC + j], o_ref(cand, mine, t), o_s.at[0], o_r.at[0],
            (p, seq_of(g * NC + j, z)),
        )

    def o_local(u, t, j):
        cand, g = u // NY, lax.rem(u, NY)
        return pltpu.make_async_copy(obuf.at[cand, t, g * NC + j], o_ref(cand, mine, t), o_r.at[0])

    def send_out(u, t):
        for j in range(NC):
            to = lax.rem(u, NY) * NC + j

            @pl.when(to == mine)
            def _(j=j):
                o_local(u, t, j).start()

            @pl.when(to != mine)
            def _(j=j):
                o_remote(u, t, j).start()

    dims = (((1,), (1,)), ((), ()))

    def lane_max(x):
        best = x[:, :HD]
        for t in range(1, x.shape[1] // HD):
            best = jnp.maximum(best, x[:, t * HD : (t + 1) * HD])
        return best

    def attend(u, g):
        cand = u // NY
        block = qbuf.at[cand, pl.ds(g * NC, NC)]
        segments = [None] + list(range(g + 1))

        def span(seg):
            return (0, NPROMPT) if seg is None else (NPROMPT + seg * SEG, SEG)

        def rows_of(t):
            return pl.ds(t * TR, TR)

        def resp_rows(seg):
            return rbuf[cand, seg].reshape(SEG, KVW)

        def score(t, seg):
            q = block[:, :, t * TW : (t + 1) * TW]
            q = jnp.concatenate(
                [q[:, :, h * HD : (h + 1) * HD].reshape(NC * ROWS, HD) for h in range(TILE)], axis=0
            )
            at, size = span(seg)
            k = kp[...] if seg is None else resp_rows(seg)[:, :HD]
            sc = lax.dot_general(q, k, dims, preferred_element_type=jnp.float32)
            if seg == g:
                sc = jnp.minimum(sc.reshape(TILE, NC * ROWS, SEG), bound[...][None]).reshape(TR, SEG)
            sbuf[rows_of(t), pl.ds(at, size)] = sc
            best = lane_max(sc)
            if seg is not None:
                best = jnp.maximum(mbuf[rows_of(t)], best)
            if seg == g:
                best = jnp.broadcast_to(jnp.max(best, axis=1, keepdims=True) * SCALE, (TR, HD))
            mbuf[rows_of(t)] = best

        def add(t, seg):
            at, size = span(seg)
            m = jnp.concatenate([mbuf[rows_of(t)]] * (size // HD), axis=1)
            w = jnp.exp2(sbuf[rows_of(t), pl.ds(at, size)] * SCALE - m).astype(jnp.bfloat16)
            if seg is None:
                v = vp[...]
            else:
                v = jnp.concatenate([resp_rows(seg)[:, HD:], jnp.ones((SEG, HD), jnp.bfloat16)], axis=1)
            part = jnp.dot(w, v, preferred_element_type=jnp.float32)
            accbuf[rows_of(t)] = part if seg is None else accbuf[rows_of(t)] + part

        def finish(t):
            acc = accbuf[rows_of(t)]
            res = (acc[:, :HD] / acc[:, HD:]).reshape(TILE, NC * ROWS, HD)
            pos = lax.broadcasted_iota(jnp.int32, (NC * ROWS, HD), 0) + (g * SEG + z * (NC * ROWS))
            alive = pos < rlen[0, cand]
            for h in range(TILE):
                piece = jnp.where(alive, res[h], 0.0).astype(jnp.bfloat16)
                obuf[cand, t, g * NC : (g + 1) * NC, :, h * HD : (h + 1) * HD] = piece.reshape(NC, ROWS, HD)
            send_out(u, t)

        for seg in segments[:-1]:
            score(0, seg)

        wait_z(lambda zz: rbuf.at[cand, g, zz], lambda zz: zr_r.at[u, zz], g == NY - 1)
        score(0, g)

        for t in range(TILES):
            for seg in segments:
                if t + 1 < TILES:
                    score(t + 1, seg)
                add(t, seg)
            finish(t)

    def unit_step(u, _):
        cand, g = u // NY, lax.rem(u, NY)
        @pl.when(u + 3 + EARLY < UNITS + 1)
        def _():
            relay_resp(u + 3 + EARLY)

        landed(qbuf.at[cand, pl.ds(g * NC, NC)], q_r.at[cand, g])
        for k in range(NY):
            @pl.when(g == k)
            def _(k=k):
                attend(u, k)
        return 0

    lax.fori_loop(0, UNITS, unit_step, 0)

    most = NY * NC - 1
    landed(qbuf.at[:, pl.ds(0, most)], q_s.at[0])
    landed(r_in.at[0, :, :, pl.ds(0, most * KVW)], r_s.at[0])

    @pl.when(p != mine)
    def _():
        landed(p_in, p_s.at[0])

    @pl.when(p == mine)
    def _():
        landed(p_in.at[pl.ds(0, NP - 1)], p_s.at[0])

    @pl.when(middle)
    def _():
        landed(pbuf, zp_s.at[0])
        landed(qbuf.at[:, pl.ds(0, 7)], zr_s.at[0])

    @pl.when(jnp.logical_not(middle))
    def _():
        landed(pbuf.at[:, pl.ds(0, 2)], zp_s.at[0])

    @pl.when(z == 0)
    def _():
        landed(qbuf.at[:, pl.ds(0, 4)], zr_s.at[0])

    @pl.when(z == NZ - 1)
    def _():
        landed(qbuf.at[:, pl.ds(0, 3)], zr_s.at[0])

    landed(obuf.at[:, :, pl.ds(0, most)], o_s.at[0])
    landed(out, o_r.at[0])


def shards(queries, resp_kv, prompt_kv, block_order, prompt_len, resp_len):
    bf16, f32 = jnp.bfloat16, jnp.float32
    dma = pltpu.SemaphoreType.DMA
    any_spec = pl.BlockSpec(memory_space=pl.ANY)
    smem = pl.BlockSpec(memory_space=pltpu.SMEM)
    return pl.pallas_call(
        kernel,
        out_shape=jax.ShapeDtypeStruct(queries.shape, bf16),
        in_specs=[any_spec] * 3 + [smem] * 3,
        out_specs=any_spec,
        scratch_shapes=[
            pltpu.VMEM((2, NY * NC, ROWS, QW), bf16),
            pltpu.VMEM((2, NY, NZ, NC, ROWS, KVW), bf16),
            pltpu.VMEM((NY, NZ, NC, CP, KVW), bf16),
            pltpu.VMEM((2, TILES, NY * NC, ROWS, TW), bf16),
            pltpu.VMEM((NPROMPT, HD), bf16),
            pltpu.VMEM((NPROMPT, KVW), bf16),
            pltpu.VMEM((RT, NPROMPT + NY * SEG), f32),
            pltpu.VMEM((RT, HD), f32),
            pltpu.VMEM((RT, KVW), f32),
            pltpu.VMEM((NC * ROWS, SEG), f32),
            dma((1,)), dma((2, NY)),
            dma((1,)), dma((NY,)),
            dma((1,)), dma((1,)),
            dma((1,)), dma((NZ,)),
            dma((1,)), dma((UNITS, NZ)),
            dma((1,)), dma((1,)),
        ],
        compiler_params=pltpu.CompilerParams(
            collective_id=0, has_side_effects=True, vmem_limit_bytes=62 * 1024 * 1024
        ),
        name="attend",
    )(queries, resp_kv, prompt_kv, block_order, prompt_len, resp_len)


def solution(mesh):
    in_specs = (
        P("prompt", None, "seq", None),
        P("prompt", None, "seq", None),
        P(None, "seq", "prompt"),
        P("prompt", None),
        P("prompt"),
        P("prompt", None),
    )
    out_specs = P("prompt", None, "seq", None)
    return jax.shard_map(shards, mesh=mesh, in_specs=in_specs, out_specs=out_specs, check_vma=False)
```
